32 devices in a mesh: row: 2 (over y), col: 16 (over z, x, core).
Axes of the slice: x: 2, y: 2, z: 4, core: 2. Of those that a mesh axis runs over, the one named last changes fastest.
Arguments:
- points: float32 [16, 4096], P(None, ('row', 'col')), may hold values from -6 to 6
- inverse_length: float32 [16], replicated, may hold values from 0.35 to 1.4
- target: float32 [4096], P(('row', 'col')), may hold values from -6 to 6
- probe_bits: int32 [15, 4096], P(None, ('row', 'col')), may hold values from 0 to 1
- leaf_inverse: float32 [4096, 128], P(('row', 'col')), may hold values from -1 to 4, as said below
- top_basis: float32 [64, 4096], P(None, ('row', 'col')), may hold values from -0.25 to 0.25
- sub_basis: float32 [64, 4096], P(None, ('row', 'col')), may hold values from -0.25 to 0.25
Outputs:
- solution: float32 [16, 4096], P(None, ('row', 'col'))
- residual: float32 [16, 4096], P(None, ('row', 'col'))
- coefficients: float32 [2, 2, 16], replicated
The draws below stay inside these ranges and needn't reach their ends.
Inputs may be any that keep to these rules, and one draw needn't show every extreme that they name: `leaf_inverse`: each leaf block is symmetric, and each of its diagonal entries exceeds the sum of the absolute values of the other entries of its row.
All inputs are finite; a program needn't handle non-finite values.
Results may differ from the reference program's by a relative error of at most 0.0003.
Values sent between devices are 32-bit elements; how exact they have to be, the bound alone decides.
A program may use at most 64 MiB of HBM per device.

```python
import math
import jax
import jax.numpy as jnp
from jax import lax

DIM = 16
RANK = 64
PROBES = 15
ITERS = 2
PTS_DEV = 128
NPTS = 4096
N_ROW = 2
N_COL = 16


def draw_leaf_inverse(key, part):
    nleaf = NPTS // PTS_DEV
    key_off = jax.random.fold_in(key, 11)
    key_diag = jax.random.fold_in(key, 12)
    raw = jax.random.uniform(key_off, (nleaf, PTS_DEV, PTS_DEV), jnp.float32, -1.0, 1.0) * (0.7 / PTS_DEV)
    sym = 0.5 * (raw + raw.transpose(0, 2, 1))
    eye = jnp.eye(PTS_DEV, dtype=jnp.float32)
    diag = jax.random.uniform(key_diag, (nleaf, PTS_DEV), jnp.float32, 0.8, 1.6)
    full = sym * (1.0 - eye)[None] + diag[:, :, None] * eye[None]
    return full.reshape(NPTS, PTS_DEV)


def set_ends(array, rng, low, top_value):
    longest = array.shape.index(max(array.shape))
    spots = []
    for shift in (0, 1):
        where = [jax.random.randint(jax.random.fold_in(rng, axis), (), 0, length) for axis, length in enumerate(array.shape)]
        where[longest] = (where[longest] + shift) % array.shape[longest]
        spots.append(tuple(where))
    return array.at[spots[0]].set(low).at[spots[1]].set(top_value)


def block_levels(own_key, extent, shards, low, largest):
    factor_of = 1.0
    for axis_at, shards_of in shards:
        heights = jax.random.uniform(jax.random.fold_in(jax.random.fold_in(own_key, 6), axis_at), (shards_of,), jnp.float32, low / len(shards), largest / len(shards))
        factor_of = factor_of * jnp.repeat(jnp.exp(heights), extent[axis_at] // shards_of).reshape((-1,) + (1,) * (len(extent) - 1 - axis_at))
    return factor_of


def gaussian(rng, extent, spread, reach, shards=(), kind=jnp.bfloat16):
    drawn = spread * jax.random.normal(rng, extent, jnp.float32)
    if shards:
        drawn = drawn * block_levels(rng, extent, shards, -0.22, 0.18)
    return jnp.clip(drawn, -reach, reach).astype(kind)


def setup_inputs(seed: int = 0) -> dict:
    splits = jax.random.split(jax.random.key(seed), 8)
    points = gaussian(splits[0], (DIM, NPTS), 1.0, 6.0, ((1, 32),), jnp.float32)
    inverse_length = jnp.clip(jnp.exp(jax.random.uniform(splits[1], (DIM,), jnp.float32, math.log(0.35), math.log(1.4))), 0.35, 1.4)
    target = gaussian(splits[2], (NPTS,), 1.0, 6.0, ((0, 32),), jnp.float32)
    probe_bits = set_ends(jax.random.randint(splits[3], (PROBES, NPTS), 0, 2), jax.random.fold_in(splits[3], 1), 0, 1).astype(jnp.int32)
    leaf_inverse = draw_leaf_inverse(jax.random.fold_in(splits[7], 71), 0)
    top_basis = gaussian(splits[5], (RANK, NPTS), (NPTS // 8) ** -0.5, 0.25, ((1, 32),), jnp.float32)
    sub_basis = gaussian(splits[6], (RANK, NPTS), (PTS_DEV * N_COL // 4) ** -0.5, 0.25, ((1, 32),), jnp.float32)
    return {"points": points, "inverse_length": inverse_length, "target": target, "probe_bits": probe_bits, "leaf_inverse": leaf_inverse, "top_basis": top_basis, "sub_basis": sub_basis}


root_five = math.sqrt(5.0)
noise_level = 0.5

def matern_block(left, right):
    left_sq = lax.optimization_barrier(jnp.sum(left * left, 0))
    right_sq = lax.optimization_barrier(jnp.sum(right * right, 0))
    cross = lax.dot_general(left, right, (((0,), (0,)), ((), ())), precision=lax.Precision.HIGHEST, preferred_element_type=jnp.float32)
    dist_sq = jnp.maximum(left_sq[:, None] + right_sq[None, :] - 2.0 * cross, 0.0)
    dist = jnp.sqrt(dist_sq)
    return (1.0 + root_five * dist + 5.0 / 3.0 * dist_sq) * jnp.exp(-root_five * dist)

def apply_kernel(scaled, vectors):
    blocks = scaled.reshape(scaled.shape[0], NPTS // PTS_DEV, PTS_DEV).transpose(1, 0, 2)

    def one_block(block_pts):
        kmat = matern_block(scaled, block_pts)
        return jnp.dot(vectors, kmat, precision=lax.Precision.HIGHEST, preferred_element_type=jnp.float32)
    out = lax.map(one_block, blocks)
    return out.transpose(1, 0, 2).reshape(vectors.shape) + noise_level * vectors

def apply_precond(vectors, leaf_inverse, top_basis, sub_basis):
    cols = vectors.shape[0]
    nleaf = NPTS // PTS_DEV
    leaves = leaf_inverse.reshape(nleaf, PTS_DEV, PTS_DEV)
    pieces = vectors.reshape(cols, nleaf, PTS_DEV)
    result = jnp.einsum('blm,cbm->cbl', leaves, pieces, precision=lax.Precision.HIGHEST).reshape(cols, NPTS)
    top_coef = jnp.dot(top_basis, vectors.T, precision=lax.Precision.HIGHEST, preferred_element_type=jnp.float32)
    result = result + jnp.dot(top_coef.T, top_basis, precision=lax.Precision.HIGHEST, preferred_element_type=jnp.float32)
    sub_view = sub_basis.reshape(RANK, N_ROW, NPTS // N_ROW)
    vec_view = vectors.reshape(cols, N_ROW, NPTS // N_ROW)
    sub_coef = jnp.einsum('knm,cnm->nkc', sub_view, vec_view, precision=lax.Precision.HIGHEST)
    result = result + jnp.einsum('nkc,knm->cnm', sub_coef, sub_view, precision=lax.Precision.HIGHEST).reshape(cols, NPTS)
    return result

def reference(points, inverse_length, target, probe_bits, leaf_inverse, top_basis, sub_basis):
    scaled = points * inverse_length[:, None]
    signs = 2.0 * probe_bits.astype(jnp.float32) - 1.0
    rhs = jnp.concatenate([target[None, :], signs], axis=0)
    solution = jnp.zeros_like(rhs)
    residual = rhs
    precond = apply_precond(residual, leaf_inverse, top_basis, sub_basis)
    direction = precond
    rz_now = lax.optimization_barrier(jnp.sum(residual * precond, 1))
    alphas = []
    betas = []
    for step in range(ITERS):
        image = apply_kernel(scaled, direction)
        alpha = rz_now / lax.optimization_barrier(jnp.sum(direction * image, 1))
        solution = solution + alpha[:, None] * direction
        residual = residual - alpha[:, None] * image
        precond = apply_precond(residual, leaf_inverse, top_basis, sub_basis)
        rz_next = lax.optimization_barrier(jnp.sum(residual * precond, 1))
        beta = rz_next / rz_now
        direction = precond + beta[:, None] * direction
        rz_now = rz_next
        alphas.append(alpha)
        betas.append(beta)
    coefficients = jnp.stack([jnp.stack(alphas), jnp.stack(betas)])
    return (solution, residual, coefficients)
```

```python
import functools
import math

import jax
import jax.numpy as jnp
from jax import lax
from jax.experimental import pallas as pl
from jax.experimental.pallas import tpu as pltpu
from jax.sharding import PartitionSpec as P

ITERS = 2
STATS = 8
MESH = pl.DeviceIdType.MESH
F32 = jnp.float32
BF16 = jnp.bfloat16

root_five = math.sqrt(5.0)
noise_level = 0.5


def halves(x):
    hi = x.astype(BF16)
    return hi, (x - hi.astype(F32)).astype(BF16)


def thirds(x):
    hi = x.astype(BF16)
    rest = x - hi.astype(F32)
    mid = rest.astype(BF16)
    return hi, mid, (rest - mid.astype(F32)).astype(BF16)


def dot_nn(a, b):
    return lax.dot_general(a, b, (((1,), (0,)), ((), ())), preferred_element_type=F32)


def dot_nt(a, b):
    return lax.dot_general(a, b, (((1,), (1,)), ((), ())), preferred_element_type=F32)


def fold(out):
    rows, width = out.shape[0] // 2, out.shape[1] // 2
    return (
        (out[rows:, width:] + out[:rows, width:]) + out[rows:, :width]
    ) + out[:rows, :width]


def stacked(x):
    return jnp.concatenate(halves(x), axis=0)


def kernel(
    n_row,
    n_col,
    rank,
    points_ref,
    length_ref,
    target_ref,
    bits_ref,
    leaf_ref,
    top_ref,
    sub_ref,
    sol_ref,
    res_ref,
    coef_ref,
    rhs_ref,
    pts_ref,
    first_ref,
    dir_ref,
    curv_ref,
    next_ref,
    last_ref,
    kmat_ref,
    send_sem,
    recv_sem,
):
    n = n_row * n_col
    row, col = lax.axis_index("row"), lax.axis_index("col")
    me = row * n_col + col
    cols, own = rhs_ref.shape
    dim = points_ref.shape[0]

    def peer(t):
        other = lax.rem(me + t, n)
        return other // n_col, lax.rem(other, n_col)

    barrier = pltpu.get_barrier_semaphore()

    def greet(t, carry):
        pl.semaphore_signal(barrier, inc=1, device_id=peer(t), device_id_type=MESH)
        return carry

    lax.fori_loop(1, n, greet, 0)

    def send(buf, at):
        def one(t, carry):
            pltpu.make_async_remote_copy(
                src_ref=buf.at[me],
                dst_ref=buf.at[me],
                send_sem=send_sem.at[at],
                recv_sem=recv_sem.at[at],
                device_id=peer(t),
                device_id_type=MESH,
            ).start()
            return carry

        lax.fori_loop(1, n, one, 0)

    def everyone(buf, at):
        return pltpu.make_async_remote_copy(
            src_ref=buf.at[pl.ds(0, n - 1)],
            dst_ref=buf.at[pl.ds(0, n - 1)],
            send_sem=send_sem.at[at],
            recv_sem=recv_sem.at[at],
            device_id=peer(1),
            device_id_type=MESH,
        )

    eye = lax.broadcasted_iota(jnp.int32, (cols, own), 0) == lax.broadcasted_iota(
        jnp.int32, (cols, own), 1
    )
    stat_row = lax.broadcasted_iota(jnp.int32, (STATS, own), 0)
    is_top = lax.broadcasted_iota(jnp.int32, (cols, 2 * rank), 1) < rank

    def to_row(column):
        return jnp.sum(jnp.where(eye, column, 0.0), axis=0, keepdims=True)

    def to_col(line):
        return jnp.sum(jnp.where(eye, line, 0.0), axis=1, keepdims=True)

    def stats(*columns):
        out = jnp.zeros((STATS, own), F32)
        for at, column in enumerate(columns):
            out = jnp.where(stat_row == at, to_row(column), out)
        return out

    def dots(a, b):
        return jnp.sum(a * b, axis=1, keepdims=True)

    rhs_ref[0:1, :] = target_ref[...]
    rhs_ref[1:cols, :] = 2.0 * bits_ref[...].astype(F32) - 1.0
    rhs = rhs_ref[...]
    inverse = jnp.sum(
        jnp.where(
            lax.broadcasted_iota(jnp.int32, (dim, dim), 0)
            == lax.broadcasted_iota(jnp.int32, (dim, dim), 1),
            length_ref[...],
            0.0,
        ),
        axis=1,
        keepdims=True,
    )
    scaled = points_ref[...] * inverse
    basis = jnp.concatenate([top_ref[...], sub_ref[...]], axis=0)
    basis_hi, basis_lo = halves(basis)
    basis_tall = jnp.concatenate([basis_hi, basis_lo], axis=0)
    basis_wide = jnp.concatenate([basis_hi, basis_lo], axis=1)
    leaf_tall = stacked(leaf_ref[...])

    def project(v):
        return fold(dot_nt(stacked(v), basis_tall))

    def expand(c):
        return fold(dot_nn(stacked(c), basis_wide))

    def leaf(v):
        return fold(dot_nt(stacked(v), leaf_tall))

    def by_subtree(buf):
        sums = []
        for i in range(n_row):
            def add(j, acc):
                return acc + buf[i * n_col + j]

            sums.append(
                lax.fori_loop(1, n_col, add, buf[i * n_col], unroll=min(n_col - 1, 15))
            )
        return sums

    def own_coef(parts):
        mine = parts[0]
        for i in range(1, n_row):
            mine = jnp.where(row == i, parts[i], mine)
        return jnp.where(is_top, sum(parts[1:], parts[0]), mine)

    def level_product(parts):
        total = sum(parts[1:], parts[0])
        squares = jnp.where(is_top, total * total, 0.0)
        for part in parts:
            squares = squares + jnp.where(is_top, 0.0, part * part)
        return jnp.sum(squares, axis=1, keepdims=True)

    def stat_sum(buf):
        def add(j, acc):
            return acc + buf[j, cols:, :]

        return lax.fori_loop(1, n, add, buf[0, cols:, :], unroll=min(n - 1, 31))

    first_ref[me] = project(rhs)
    pts_ref[me] = scaled
    pl.semaphore_wait(barrier, n - 1)
    send(first_ref, 0)
    send(pts_ref, 1)

    leaf_res = leaf(rhs)
    everyone(first_ref, 0).wait_recv()
    parts = by_subtree(first_ref)
    direction = leaf_res + expand(own_coef(parts))
    dir_ref[me, 0:cols, :] = direction
    dir_ref[me, cols:, :] = stats(dots(rhs, leaf_res))
    send(dir_ref, 2)

    def norm_rows(sq, first):
        pieces = [p.astype(F32) for p in thirds(sq)]
        line = lax.broadcasted_iota(jnp.int32, (16, sq.shape[1]), 0)
        out = jnp.where((line >= 3 - 3 * first) & (line < 6 - 3 * first), 1.0, 0.0)
        for at, piece in enumerate(pieces):
            out = jnp.where(line == 3 * first + at, piece, out)
        return out.astype(BF16)

    def features(x, order, first):
        pieces = thirds(x)
        sq = jnp.sum(x * x, axis=0, keepdims=True)
        return [pieces[at] for at in order], norm_rows(sq, first)

    own_parts, own_norm = features(scaled, (0, 0, 0, 1, 1, 2), 0)
    own_feat = jnp.concatenate([-2.0 * p.astype(F32) for p in own_parts] + [own_norm.astype(F32)], axis=0)
    own_feat = own_feat.T.astype(BF16)
    everyone(pts_ref, 1).wait_recv()

    def build(p, carry):
        pair = jnp.concatenate([pts_ref[2 * p], pts_ref[2 * p + 1]], axis=1)
        far_parts, far_norm = features(pair, (0, 1, 2, 0, 1, 0), 1)
        far_feat = jnp.concatenate(far_parts + [far_norm], axis=0)
        five_sq = jnp.maximum(5.0 * dot_nn(own_feat, far_feat), 1e-30)
        dist = five_sq * lax.rsqrt(five_sq)
        value = (1.0 + dist + five_sq * (1.0 / 3.0)) * jnp.exp(-dist)
        hi, lo = halves(value)
        kmat_ref[p, 0:own, :] = hi
        kmat_ref[p, own:, :] = lo
        return carry

    lax.fori_loop(0, n // 2, build, 0, unroll=2)

    def apply_kernel(buf):
        def add(p, acc):
            pair = jnp.concatenate([buf[2 * p, 0:cols, :], buf[2 * p + 1, 0:cols, :]], axis=1)
            return acc + dot_nt(stacked(pair), kmat_ref[p])

        zero = jnp.zeros((2 * cols, 2 * own), F32)
        return fold(lax.fori_loop(0, n // 2, add, zero, unroll=min(n // 2, 16)))

    everyone(dir_ref, 2).wait_recv()
    rz_now = to_col(stat_sum(dir_ref)[0:1]) + level_product(parts)
    image = apply_kernel(dir_ref) + noise_level * direction
    curv_ref[me, 0:cols, :] = project(image)
    curv_ref[me, cols:, :] = stats(dots(direction, image))
    send(curv_ref, 3)
    leaf_image = leaf(image)
    everyone(curv_ref, 3).wait_recv()
    sums = by_subtree(curv_ref)
    curv = to_col(sum([s[cols : cols + 1] for s in sums[1:]], sums[0][cols : cols + 1]))
    alpha_0 = rz_now / curv
    answer = alpha_0 * direction
    residual = rhs - alpha_0 * image
    leaf_res = leaf_res - alpha_0 * leaf_image
    parts = [a - alpha_0 * s[0:cols] for a, s in zip(parts, sums)]
    precond = leaf_res + expand(own_coef(parts))
    leaf_prod = dots(residual, leaf_res)
    next_ref[me, 0:cols, :] = precond
    next_ref[me, cols:, :] = stats(leaf_prod)
    send(next_ref, 4)

    everyone(next_ref, 4).wait_recv()
    leaf_total = to_col(stat_sum(next_ref)[0:1])
    rz_next = leaf_total + level_product(parts)
    beta_0 = rz_next / rz_now
    rz_now = rz_next
    direction = precond + beta_0 * direction
    image = apply_kernel(next_ref) + noise_level * precond + beta_0 * image
    leaf_image = leaf(image)
    last_ref[me, 0:cols, :] = project(image)
    last_ref[me, cols:, :] = stats(
        dots(direction, image), dots(image, leaf_res), dots(image, leaf_image)
    )
    send(last_ref, 5)
    everyone(last_ref, 5).wait_recv()
    sums = by_subtree(last_ref)
    stat = sum([s[cols:] for s in sums[1:]], sums[0][cols:])
    alpha_1 = rz_now / to_col(stat[0:1])
    sol_ref[...] = answer + alpha_1 * direction
    res_ref[...] = residual - alpha_1 * image
    parts = [a - alpha_1 * s[0:cols] for a, s in zip(parts, sums)]
    leaf_last = leaf_total - alpha_1 * (2.0 * to_col(stat[1:2]) - alpha_1 * to_col(stat[2:3]))
    beta_1 = (leaf_last + level_product(parts)) / rz_now
    for i, (alpha, beta) in enumerate(((alpha_0, beta_0), (alpha_1, beta_1))):
        coef_ref[0, i : i + 1, :] = to_row(alpha)[:, 0:cols]
        coef_ref[1, i : i + 1, :] = to_row(beta)[:, 0:cols]
    for at, buf in enumerate((first_ref, pts_ref, dir_ref, curv_ref, next_ref, last_ref)):
        everyone(buf, at).wait_send()


def on_device(n_row, n_col, points, inverse_length, target, probe_bits, leaf_inverse, top_basis, sub_basis):
    n = n_row * n_col
    dim, own = points.shape
    cols = probe_bits.shape[0] + 1
    vmem = pl.BlockSpec(memory_space=pltpu.VMEM)
    block = (n, cols, own)
    message = (n, cols + STATS, own)
    return pl.pallas_call(
        functools.partial(kernel, n_row, n_col, top_basis.shape[0]),
        out_shape=(
            jax.ShapeDtypeStruct((cols, own), F32),
            jax.ShapeDtypeStruct((cols, own), F32),
            jax.ShapeDtypeStruct((2, ITERS, cols), F32),
        ),
        in_specs=[vmem] * 7,
        out_specs=(vmem, vmem, vmem),
        scratch_shapes=[
            pltpu.VMEM((cols, own), F32),
            pltpu.VMEM((n, dim, own), F32),
            pltpu.VMEM((n, cols, 2 * top_basis.shape[0]), F32),
            pltpu.VMEM(message, F32),
            pltpu.VMEM(message, F32),
            pltpu.VMEM(message, F32),
            pltpu.VMEM(message, F32),
            pltpu.VMEM((n // 2, 2 * own, 2 * own), BF16),
            pltpu.SemaphoreType.DMA((6,)),
            pltpu.SemaphoreType.DMA((6,)),
        ],
        compiler_params=pltpu.CompilerParams(
            collective_id=0, has_side_effects=True, vmem_limit_bytes=48 * 1024 * 1024
        ),
    )(
        points,
        inverse_length.reshape(1, dim),
        target.reshape(1, own),
        probe_bits,
        leaf_inverse,
        top_basis,
        sub_basis,
    )


def solution(mesh):
    return jax.shard_map(
        functools.partial(on_device, mesh.shape["row"], mesh.shape["col"]),
        mesh=mesh,
        in_specs=(
            P(None, ("row", "col")),
            P(),
            P(("row", "col")),
            P(None, ("row", "col")),
            P(("row", "col"), None),
            P(None, ("row", "col")),
            P(None, ("row", "col")),
        ),
        out_specs=(P(None, ("row", "col")), P(None, ("row", "col")), P()),
        check_vma=False,
    )
```

```python
import functools
import math

import jax
import jax.numpy as jnp
from jax import lax
from jax.experimental import pallas as pl
from jax.experimental.pallas import tpu as pltpu
from jax.sharding import PartitionSpec as P

ITERS = 2
STATS = 8
MESH = pl.DeviceIdType.MESH
F32 = jnp.float32
BF16 = jnp.bfloat16

root_five = math.sqrt(5.0)
noise_level = 0.5


def halves(x):
    hi = x.astype(BF16)
    return hi, (x - hi.astype(F32)).astype(BF16)


def thirds(x):
    hi = x.astype(BF16)
    rest = x - hi.astype(F32)
    mid = rest.astype(BF16)
    return hi, mid, (rest - mid.astype(F32)).astype(BF16)


def dot_nn(a, b):
    return lax.dot_general(a, b, (((1,), (0,)), ((), ())), preferred_element_type=F32)


def dot_nt(a, b):
    return lax.dot_general(a, b, (((1,), (1,)), ((), ())), preferred_element_type=F32)


def fold(out):
    rows, width = out.shape[0] // 2, out.shape[1] // 2
    return (
        (out[rows:, width:] + out[:rows, width:]) + out[rows:, :width]
    ) + out[:rows, :width]


def stacked(x):
    return jnp.concatenate(halves(x), axis=0)


def kernel(
    n_row,
    n_col,
    low,
    rank,
    points_hbm,
    length_hbm,
    target_hbm,
    bits_hbm,
    leaf_hbm,
    top_hbm,
    sub_hbm,
    sol_ref,
    res_ref,
    coef_ref,
    points_ref,
    length_ref,
    bits_ref,
    leaf_ref,
    basis_ref,
    target_ref,
    rhs_ref,
    pts_line_ref,
    pts_plane_ref,
    line_ref,
    plane_ref,
    out_ref,
    kmat_ref,
    load_sem,
    send_sem,
    recv_sem,
):
    n_line = n_col // low
    n_plane = n_row * low
    row, col = lax.axis_index("row"), lax.axis_index("col")
    in_line = col // low
    lowest = lax.rem(col, low)
    in_plane = row * low + lowest
    cols, own = rhs_ref.shape
    dim = points_ref.shape[0]

    def line_peer(t):
        return row, lax.rem(in_line + t, n_line) * low + lowest

    def plane_slot(t):
        return lax.rem(in_plane + t, n_plane)

    def plane_peer(t):
        other = plane_slot(t)
        return other // low, in_line * low + lax.rem(other, low)

    loads = [
        pltpu.make_async_copy(src, dst, load_sem.at[at])
        for at, (src, dst) in enumerate(
            (
                (points_hbm, points_ref),
                (length_hbm, length_ref),
                (target_hbm, target_ref),
                (bits_hbm, bits_ref),
                (top_hbm, basis_ref.at[pl.ds(0, rank)]),
                (sub_hbm, basis_ref.at[pl.ds(rank, rank)]),
                (leaf_hbm, leaf_ref),
            )
        )
    ]
    for load in loads:
        load.start()

    barrier = pltpu.get_barrier_semaphore()
    for t in range(1, n_line):
        pl.semaphore_signal(barrier, inc=1, device_id=line_peer(t), device_id_type=MESH)
    for t in range(1, n_plane):
        pl.semaphore_signal(barrier, inc=1, device_id=plane_peer(t), device_id_type=MESH)

    def remote(src, dst, at, device):
        return pltpu.make_async_remote_copy(
            src_ref=src,
            dst_ref=dst,
            send_sem=send_sem.at[at],
            recv_sem=recv_sem.at[at],
            device_id=device,
            device_id_type=MESH,
        )

    def send_line(buf, at):
        for t in range(1, n_line):
            remote(buf.at[in_line], buf.at[in_line], at, line_peer(t)).start()

    def send_plane(buf, at):
        for t in range(1, n_plane):
            remote(buf.at[in_plane], buf.at[in_plane], at, plane_peer(t)).start()

    def all_line(buf, at):
        some = buf.at[pl.ds(0, n_line - 1)]
        return remote(some, some, at, line_peer(1))

    def all_plane(buf, at):
        some = buf.at[pl.ds(0, n_plane - 1)]
        return remote(some, some, at, plane_peer(1))

    eye = lax.broadcasted_iota(jnp.int32, (cols, own), 0) == lax.broadcasted_iota(
        jnp.int32, (cols, own), 1
    )
    stat_row = lax.broadcasted_iota(jnp.int32, (STATS, own), 0)
    is_top = lax.broadcasted_iota(jnp.int32, (cols, 2 * rank), 1) < rank

    def to_row(column):
        return jnp.sum(jnp.where(eye, column, 0.0), axis=0, keepdims=True)

    def to_col(line):
        return jnp.sum(jnp.where(eye, line, 0.0), axis=1, keepdims=True)

    def stats(*columns):
        out = jnp.zeros((STATS, own), F32)
        for at, column in enumerate(columns):
            out = jnp.where(stat_row == at, to_row(column), out)
        return out

    def dots(a, b):
        return jnp.sum(a * b, axis=1, keepdims=True)

    for load in loads[:4]:
        load.wait()
    rhs_ref[0:1, :] = target_ref[...]
    rhs_ref[1:cols, :] = 2.0 * bits_ref[...].astype(F32) - 1.0
    rhs = rhs_ref[...]
    inverse = jnp.sum(
        jnp.where(
            lax.broadcasted_iota(jnp.int32, (dim, dim), 0)
            == lax.broadcasted_iota(jnp.int32, (dim, dim), 1),
            length_ref[...],
            0.0,
        ),
        axis=1,
        keepdims=True,
    )
    scaled = points_ref[...] * inverse
    pts_line_ref[in_line] = scaled
    pts_plane_ref[in_plane] = scaled
    for load in loads[4:]:
        load.wait()
    basis_hi, basis_lo = halves(basis_ref[...])
    basis_tall = jnp.concatenate([basis_hi, basis_lo], axis=0)
    basis_wide = jnp.concatenate([basis_hi, basis_lo], axis=1)
    leaf_tall = stacked(leaf_ref[...])

    def project(v):
        return fold(dot_nt(stacked(v), basis_tall))

    def expand(c):
        return fold(dot_nn(stacked(c), basis_wide))

    def leaf(v):
        return fold(dot_nt(stacked(v), leaf_tall))

    def total(buf, first, count):
        out = buf[first]
        for i in range(first + 1, first + count):
            out = out + buf[i]
        return out

    def by_subtree(at):
        send_line(line_ref.at[at], 2 * at)
        yield
        all_line(line_ref.at[at], 2 * at).wait_recv()
        plane_ref[at, in_plane] = total(line_ref.at[at], 0, n_line)
        send_plane(plane_ref.at[at], 2 * at + 1)
        yield
        all_plane(plane_ref.at[at], 2 * at + 1).wait_recv()
        yield [total(plane_ref.at[at], i * low, low) for i in range(n_row)]

    def own_coef(parts):
        mine = parts[0]
        for i in range(1, n_row):
            mine = jnp.where(row == i, parts[i], mine)
        return jnp.where(is_top, sum(parts[1:], parts[0]), mine)

    def level_product(parts):
        every = sum(parts[1:], parts[0])
        squares = jnp.where(is_top, every * every, 0.0)
        for part in parts:
            squares = squares + jnp.where(is_top, 0.0, part * part)
        return jnp.sum(squares, axis=1, keepdims=True)

    line_ref[0, in_line, 0:cols, :] = project(rhs)
    leaf_res = leaf(rhs)
    line_ref[0, in_line, cols:, :] = stats(dots(rhs, leaf_res))
    pl.semaphore_wait(barrier, n_line + n_plane - 2)
    reduce = by_subtree(0)
    next(reduce)
    send_line(pts_line_ref, 10)
    send_plane(pts_plane_ref, 11)
    next(reduce)

    def norm_rows(sq, first):
        pieces = [p.astype(F32) for p in thirds(sq)]
        line = lax.broadcasted_iota(jnp.int32, (16, sq.shape[1]), 0)
        out = jnp.where((line >= 3 - 3 * first) & (line < 6 - 3 * first), 1.0, 0.0)
        for at, piece in enumerate(pieces):
            out = jnp.where(line == 3 * first + at, piece, out)
        return out.astype(BF16)

    def features(x, order, first):
        pieces = thirds(x)
        sq = jnp.sum(x * x, axis=0, keepdims=True)
        return [pieces[at] for at in order], norm_rows(sq, first)

    all_line(pts_line_ref, 10).wait_recv()
    sources = jnp.concatenate([pts_line_ref[i] for i in range(n_line)], axis=1)
    src_parts, src_norm = features(sources, (0, 0, 0, 1, 1, 2), 0)
    src_feat = jnp.concatenate(
        [-2.0 * p.astype(F32) for p in src_parts] + [src_norm.astype(F32)], axis=0
    ).T.astype(BF16)
    all_plane(pts_plane_ref, 11).wait_recv()

    sums = next(reduce)
    stat = sum([s[cols:] for s in sums[1:]], sums[0][cols:])
    parts = [s[0:cols] for s in sums]
    rz_now = to_col(stat[0:1]) + level_product(parts)
    direction = leaf_res + expand(own_coef(parts))
    line_ref[1, in_line, 0:cols, :] = direction
    line_ref[1, in_line, cols:, :] = jnp.zeros((STATS, own), F32)
    send_line(line_ref.at[1], 2)

    def build(q, carry):
        pair = jnp.concatenate(
            [pts_plane_ref[plane_slot(2 * q + 1)], pts_plane_ref[plane_slot(2 * q + 2)]], axis=1
        )
        far_parts, far_norm = features(pair, (0, 1, 2, 0, 1, 0), 1)
        far_feat = jnp.concatenate(far_parts + [far_norm], axis=0)
        for i in range(n_line):
            some = src_feat[i * own : (i + 1) * own]
            five_sq = jnp.maximum(5.0 * dot_nn(some, far_feat), 1e-30)
            dist = five_sq * lax.rsqrt(five_sq)
            value = (1.0 + dist + five_sq * (1.0 / 3.0)) * jnp.exp(-dist)
            hi, lo = halves(value)
            kmat_ref[q, i * own : (i + 1) * own, 0 : 2 * own] = hi
            kmat_ref[q, i * own : (i + 1) * own, 2 * own :] = lo
        return carry

    lax.fori_loop(0, n_plane // 2, build, 0)

    def apply_kernel(at):
        all_line(line_ref.at[at], 2 * at).wait_recv()
        mine = stacked(
            jnp.concatenate([line_ref[at, i, 0:cols, :] for i in range(n_line)], axis=1)
        )
        stat = total(line_ref.at[at, :, pl.ds(cols, STATS)], 0, n_line)
        for q in range(n_plane // 2):
            both = fold(dot_nn(mine, kmat_ref[q]))
            for half in range(2):
                t = 2 * q + 1 + half
                block = both[:, half * own : (half + 1) * own]
                if t == n_plane:
                    plane_ref[at, in_plane, 0:cols, :] = block
                    plane_ref[at, in_plane, cols:, :] = stat
                    continue
                slot = at // 2 * (n_plane - 1) + t - 1
                out_ref[slot, 0:cols, :] = block
                out_ref[slot, cols:, :] = stat
                remote(
                    out_ref.at[slot], plane_ref.at[at, in_plane], 2 * at + 1, plane_peer(t)
                ).start()
        all_plane(plane_ref.at[at], 2 * at + 1).wait_recv()
        both = total(plane_ref.at[at], 0, n_plane)
        return both[0:cols], both[cols:]

    image, _ = apply_kernel(1)
    image = image + noise_level * direction
    line_ref[2, in_line, 0:cols, :] = project(image)
    line_ref[2, in_line, cols:, :] = stats(dots(direction, image))
    reduce = by_subtree(2)
    next(reduce)
    leaf_image = leaf(image)
    next(reduce)
    sums = next(reduce)
    stat = sum([s[cols:] for s in sums[1:]], sums[0][cols:])
    alpha_0 = rz_now / to_col(stat[0:1])
    residual = rhs - alpha_0 * image
    leaf_res = leaf_res - alpha_0 * leaf_image
    parts = [a - alpha_0 * s[0:cols] for a, s in zip(parts, sums)]
    precond = leaf_res + expand(own_coef(parts))
    line_ref[3, in_line, 0:cols, :] = precond
    line_ref[3, in_line, cols:, :] = stats(dots(residual, leaf_res))
    send_line(line_ref.at[3], 6)
    answer = alpha_0 * direction
    levels = level_product(parts)

    product, stat = apply_kernel(3)
    leaf_total = to_col(stat[0:1])
    rz_next = leaf_total + levels
    beta_0 = rz_next / rz_now
    rz_now = rz_next
    direction = precond + beta_0 * direction
    image = product + noise_level * precond + beta_0 * image
    leaf_image = leaf(image)
    line_ref[4, in_line, 0:cols, :] = project(image)
    line_ref[4, in_line, cols:, :] = stats(
        dots(direction, image), dots(image, leaf_res), dots(image, leaf_image)
    )
    reduce = by_subtree(4)
    next(reduce)
    next(reduce)
    sums = next(reduce)
    stat = sum([s[cols:] for s in sums[1:]], sums[0][cols:])
    alpha_1 = rz_now / to_col(stat[0:1])
    sol_ref[...] = answer + alpha_1 * direction
    res_ref[...] = residual - alpha_1 * image
    parts = [a - alpha_1 * s[0:cols] for a, s in zip(parts, sums)]
    leaf_last = leaf_total - alpha_1 * (2.0 * to_col(stat[1:2]) - alpha_1 * to_col(stat[2:3]))
    beta_1 = (leaf_last + level_product(parts)) / rz_now
    for i, (alpha, beta) in enumerate(((alpha_0, beta_0), (alpha_1, beta_1))):
        coef_ref[0, i : i + 1, :] = to_row(alpha)[:, 0:cols]
        coef_ref[1, i : i + 1, :] = to_row(beta)[:, 0:cols]
    for at in range(5):
        all_line(line_ref.at[at], 2 * at).wait_send()
        all_plane(plane_ref.at[at], 2 * at + 1).wait_send()
    all_line(pts_line_ref, 10).wait_send()
    all_plane(pts_plane_ref, 11).wait_send()


def on_device(n_row, n_col, points, inverse_length, target, probe_bits, leaf_inverse, top_basis, sub_basis):
    low = math.gcd(n_col, 4)
    n_line, n_plane = n_col // low, n_row * low
    dim, own = points.shape
    cols = probe_bits.shape[0] + 1
    rank = top_basis.shape[0]
    vmem = pl.BlockSpec(memory_space=pltpu.VMEM)
    hbm = pl.BlockSpec(memory_space=pltpu.HBM)
    message = (cols + STATS, own)
    return pl.pallas_call(
        functools.partial(kernel, n_row, n_col, low, rank),
        out_shape=(
            jax.ShapeDtypeStruct((cols, own), F32),
            jax.ShapeDtypeStruct((cols, own), F32),
            jax.ShapeDtypeStruct((2, ITERS, cols), F32),
        ),
        in_specs=[hbm] * 7,
        out_specs=(vmem, vmem, vmem),
        scratch_shapes=[
            pltpu.VMEM(points.shape, F32),
            pltpu.VMEM((1, dim), F32),
            pltpu.VMEM(probe_bits.shape, jnp.int32),
            pltpu.VMEM(leaf_inverse.shape, F32),
            pltpu.VMEM((2 * rank, own), F32),
            pltpu.VMEM((1, own), F32),
            pltpu.VMEM((cols, own), F32),
            pltpu.VMEM((n_line, dim, own), F32),
            pltpu.VMEM((n_plane, dim, own), F32),
            pltpu.VMEM((5, n_line) + message, F32),
            pltpu.VMEM((5, n_plane) + message, F32),
            pltpu.VMEM((2 * (n_plane - 1),) + message, F32),
            pltpu.VMEM((n_plane // 2, n_line * own, 4 * own), BF16),
            pltpu.SemaphoreType.DMA((7,)),
            pltpu.SemaphoreType.DMA((12,)),
            pltpu.SemaphoreType.DMA((12,)),
        ],
        compiler_params=pltpu.CompilerParams(
            collective_id=0, has_side_effects=True, vmem_limit_bytes=48 * 1024 * 1024
        ),
    )(
        points,
        inverse_length.reshape(1, dim),
        target.reshape(1, own),
        probe_bits,
        leaf_inverse,
        top_basis,
        sub_basis,
    )


def solution(mesh):
    return jax.shard_map(
        functools.partial(on_device, mesh.shape["row"], mesh.shape["col"]),
        mesh=mesh,
        in_specs=(
            P(None, ("row", "col")),
            P(),
            P(("row", "col")),
            P(None, ("row", "col")),
            P(("row", "col"), None),
            P(None, ("row", "col")),
            P(None, ("row", "col")),
        ),
        out_specs=(P(None, ("row", "col")), P(None, ("row", "col")), P()),
        check_vma=False,
    )
```

```python
import functools
import math

import jax
import jax.numpy as jnp
from jax import lax
from jax.experimental import pallas as pl
from jax.experimental.pallas import tpu as pltpu
from jax.sharding import PartitionSpec as P

ITERS = 2
STATS = 8
MESH = pl.DeviceIdType.MESH
F32 = jnp.float32
BF16 = jnp.bfloat16

root_five = math.sqrt(5.0)
noise_level = 0.5


def halves(x):
    hi = x.astype(BF16)
    return hi, (x - hi.astype(F32)).astype(BF16)


def thirds(x):
    hi = x.astype(BF16)
    rest = x - hi.astype(F32)
    mid = rest.astype(BF16)
    return hi, mid, (rest - mid.astype(F32)).astype(BF16)


def dot_nn(a, b):
    return lax.dot_general(a, b, (((1,), (0,)), ((), ())), preferred_element_type=F32)


def dot_nt(a, b):
    return lax.dot_general(a, b, (((1,), (1,)), ((), ())), preferred_element_type=F32)


def fold(out):
    rows, width = out.shape[0] // 2, out.shape[1] // 2
    return (
        (out[rows:, width:] + out[:rows, width:]) + out[rows:, :width]
    ) + out[:rows, :width]


def stacked(x):
    return jnp.concatenate(halves(x), axis=0)


def kernel(
    n_row,
    n_col,
    low,
    rank,
    points_hbm,
    length_hbm,
    target_hbm,
    bits_hbm,
    leaf_hbm,
    top_hbm,
    sub_hbm,
    sol_ref,
    res_ref,
    coef_ref,
    points_ref,
    length_ref,
    bits_ref,
    leaf_ref,
    basis_ref,
    wide_ref,
    target_ref,
    rhs_ref,
    pts_line_ref,
    pts_plane_ref,
    line_ref,
    plane_ref,
    prod_ref,
    out_ref,
    kmat_ref,
    load_sem,
    send_sem,
    recv_sem,
):
    n_high = n_col // low
    n_line, n_plane = low, n_row * n_high
    row, col = lax.axis_index("row"), lax.axis_index("col")
    high = col // low
    in_line = lax.rem(col, low)
    in_plane = row * n_high + high
    cols, own = rhs_ref.shape
    dim = points_ref.shape[0]

    def line_peer(t):
        return row, high * low + lax.rem(in_line + t, n_line)

    def plane_slot(t):
        return lax.rem(in_plane + t, n_plane)

    def plane_peer(t):
        other = plane_slot(t)
        return other // n_high, lax.rem(other, n_high) * low + in_line

    loads = [
        pltpu.make_async_copy(src, dst, load_sem.at[at])
        for at, (src, dst) in enumerate(
            (
                (points_hbm, points_ref),
                (length_hbm, length_ref),
                (target_hbm, target_ref),
                (bits_hbm, bits_ref),
                (top_hbm, basis_ref.at[in_line, pl.ds(0, rank)]),
                (sub_hbm, basis_ref.at[in_line, pl.ds(rank, rank)]),
                (leaf_hbm, leaf_ref),
            )
        )
    ]
    for load in loads:
        load.start()

    barrier = pltpu.get_barrier_semaphore()
    for t in range(1, n_line):
        pl.semaphore_signal(barrier, inc=1, device_id=line_peer(t), device_id_type=MESH)
    for t in range(1, n_plane):
        pl.semaphore_signal(barrier, inc=1, device_id=plane_peer(t), device_id_type=MESH)

    def remote(src, dst, at, device):
        return pltpu.make_async_remote_copy(
            src_ref=src,
            dst_ref=dst,
            send_sem=send_sem.at[at],
            recv_sem=recv_sem.at[at],
            device_id=device,
            device_id_type=MESH,
        )

    def send_line(buf, at):
        mine = buf.at[in_line]
        for t in range(1, n_line):
            remote(mine, mine, at, line_peer(t)).start()

    def send_plane(buf, at):
        mine = buf.at[in_plane]
        for t in range(1, n_plane):
            remote(mine, mine, at, plane_peer(t)).start()

    def all_line(buf, at):
        some = buf.at[pl.ds(0, n_line - 1)]
        return remote(some, some, at, line_peer(1))

    def all_plane(buf, at):
        some = buf.at[pl.ds(0, n_plane - 1)]
        return remote(some, some, at, plane_peer(1))

    eye = lax.broadcasted_iota(jnp.int32, (cols, own), 0) == lax.broadcasted_iota(
        jnp.int32, (cols, own), 1
    )
    stat_row = lax.broadcasted_iota(jnp.int32, (STATS, own), 0)
    is_top = lax.broadcasted_iota(jnp.int32, (cols, 2 * rank), 1) < rank

    def to_row(column):
        return jnp.sum(jnp.where(eye, column, 0.0), axis=0, keepdims=True)

    def to_col(line):
        return jnp.sum(jnp.where(eye, line, 0.0), axis=1, keepdims=True)

    def stats(*columns):
        out = jnp.zeros((STATS, own), F32)
        for at, column in enumerate(columns):
            out = jnp.where(stat_row == at, to_row(column), out)
        return out

    def dots(a, b):
        return jnp.sum(a * b, axis=1, keepdims=True)

    for load in loads[:4]:
        load.wait()
    rhs_ref[0:1, :] = target_ref[...]
    rhs_ref[1:cols, :] = 2.0 * bits_ref[...].astype(F32) - 1.0
    rhs = rhs_ref[...]
    inverse = jnp.sum(
        jnp.where(
            lax.broadcasted_iota(jnp.int32, (dim, dim), 0)
            == lax.broadcasted_iota(jnp.int32, (dim, dim), 1),
            length_ref[...],
            0.0,
        ),
        axis=1,
        keepdims=True,
    )
    scaled = points_ref[...] * inverse
    pts_line_ref[in_line] = scaled
    pts_plane_ref[in_plane] = scaled
    for load in loads[4:]:
        load.wait()
    basis_tall = stacked(basis_ref[in_line])
    leaf_tall = stacked(leaf_ref[...])

    def project(v):
        return fold(dot_nt(stacked(v), basis_tall))

    def expand(c):
        return fold(dot_nn(stacked(c), wide_ref[...]))

    def leaf(v):
        return fold(dot_nt(stacked(v), leaf_tall))

    def total(buf, first, count):
        out = buf[first]
        for i in range(first + 1, first + count):
            out = out + buf[i]
        return out

    def by_subtree(at, length):
        message = line_ref.at[at, :, pl.ds(0, length)]
        send_line(message, 2 * at)
        yield
        all_line(message, 2 * at).wait_recv()
        plane_ref[at, in_plane] = total(line_ref.at[at, :, pl.ds(0, cols + STATS)], 0, n_line)
        send_plane(plane_ref.at[at], 2 * at + 1)
        yield
        all_plane(plane_ref.at[at], 2 * at + 1).wait_recv()
        sums = [total(plane_ref.at[at], i * n_high, n_high) for i in range(n_row)]
        yield [s[0:cols] for s in sums], sum([s[cols:] for s in sums[1:]], sums[0][cols:])

    def put(at, vector, columns, *more):
        line_ref[at, in_line, 0:cols, :] = project(vector)
        line_ref[at, in_line, cols : cols + STATS, :] = stats(*columns)
        for i, part in enumerate(more):
            first = cols + STATS + i * cols
            line_ref[at, in_line, first : first + cols, :] = part

    def of_line(at, which):
        first = cols + STATS + which * cols
        return jnp.concatenate(
            [line_ref[at, i, first : first + cols, :] for i in range(n_line)], axis=1
        )

    def pick(lanes):
        mine = lanes[:, 0:own]
        for i in range(1, n_line):
            mine = jnp.where(in_line == i, lanes[:, i * own : (i + 1) * own], mine)
        return mine

    def own_coef(parts):
        mine = parts[0]
        for i in range(1, n_row):
            mine = jnp.where(row == i, parts[i], mine)
        return jnp.where(is_top, sum(parts[1:], parts[0]), mine)

    def level_product(parts):
        every = sum(parts[1:], parts[0])
        squares = jnp.where(is_top, every * every, 0.0)
        for part in parts:
            squares = squares + jnp.where(is_top, 0.0, part * part)
        return jnp.sum(squares, axis=1, keepdims=True)

    long = cols + STATS + 2 * cols
    leaf_res = leaf(rhs)
    put(0, rhs, (dots(rhs, leaf_res),), leaf_res, rhs)
    pl.semaphore_wait(barrier, n_line + n_plane - 2)
    reduce = by_subtree(0, long)
    next(reduce)
    send_line(pts_line_ref, 6)
    send_plane(pts_plane_ref, 7)
    send_line(basis_ref, 8)
    next(reduce)

    def norm_rows(sq, first):
        pieces = [p.astype(F32) for p in thirds(sq)]
        line = lax.broadcasted_iota(jnp.int32, (16, sq.shape[1]), 0)
        out = jnp.where((line >= 3 - 3 * first) & (line < 6 - 3 * first), 1.0, 0.0)
        for at, piece in enumerate(pieces):
            out = jnp.where(line == 3 * first + at, piece, out)
        return out.astype(BF16)

    def features(x, order, first):
        pieces = thirds(x)
        sq = jnp.sum(x * x, axis=0, keepdims=True)
        return [pieces[at] for at in order], norm_rows(sq, first)

    all_line(pts_line_ref, 6).wait_recv()
    sources = jnp.concatenate([pts_line_ref[i] for i in range(n_line)], axis=1)
    src_parts, src_norm = features(sources, (0, 0, 0, 1, 1, 2), 0)
    src_feat = jnp.concatenate(
        [-2.0 * p.astype(F32) for p in src_parts] + [src_norm.astype(F32)], axis=0
    ).T.astype(BF16)
    all_plane(pts_plane_ref, 7).wait_recv()

    def build(q, carry):
        pair = jnp.concatenate(
            [pts_plane_ref[plane_slot(2 * q + 1)], pts_plane_ref[plane_slot(2 * q + 2)]], axis=1
        )
        far_parts, far_norm = features(pair, (0, 1, 2, 0, 1, 0), 1)
        far_feat = jnp.concatenate(far_parts + [far_norm], axis=0)
        for i in range(n_line):
            some = src_feat[i * own : (i + 1) * own]
            five_sq = jnp.maximum(5.0 * dot_nn(some, far_feat), 1e-30)
            dist = five_sq * lax.rsqrt(five_sq)
            value = (1.0 + dist + five_sq * (1.0 / 3.0)) * jnp.exp(-dist)
            hi, lo = halves(value)
            kmat_ref[q, i * own : (i + 1) * own, 0 : 2 * own] = hi
            kmat_ref[q, i * own : (i + 1) * own, 2 * own :] = lo
        return carry

    lax.fori_loop(0, n_plane // 2, build, 0)

    all_line(basis_ref, 8).wait_recv()
    for i in range(n_line):
        hi, lo = halves(basis_ref[i])
        wide_ref[:, i * own : (i + 1) * own] = hi
        wide_ref[:, (n_line + i) * own : (n_line + i + 1) * own] = lo

    def apply_kernel(which, vectors, stat):
        at = 9 + which
        mine = stacked(vectors)
        length = cols if stat is None else cols + STATS
        inbox = prod_ref.at[which, :, pl.ds(0, length)]
        for q in range(n_plane // 2):
            both = fold(dot_nn(mine, kmat_ref[q]))
            for half in range(2):
                t = 2 * q + 1 + half
                block = both[:, half * own : (half + 1) * own]
                if t == n_plane:
                    prod_ref[which, in_plane, 0:cols, :] = block
                    if stat is not None:
                        prod_ref[which, in_plane, cols:, :] = stat
                    continue
                slot = which * (n_plane - 1) + t - 1
                out_ref[slot, 0:cols, :] = block
                if stat is not None:
                    out_ref[slot, cols:, :] = stat
                remote(
                    out_ref.at[slot, pl.ds(0, length)],
                    inbox.at[in_plane],
                    at,
                    plane_peer(t),
                ).start()
        all_plane(inbox, at).wait_recv()
        return total(inbox, 0, n_plane)

    parts, stat = next(reduce)
    rz_now = to_col(stat[0:1]) + level_product(parts)
    leaf_lanes = of_line(0, 0)
    lanes = leaf_lanes + expand(own_coef(parts))
    direction = pick(lanes)

    image = apply_kernel(0, lanes, None) + noise_level * direction
    leaf_image = leaf(image)
    put(1, image, (dots(direction, image),), leaf_image, image)
    reduce = by_subtree(1, long)
    next(reduce)
    next(reduce)
    sums, stat = next(reduce)
    alpha_0 = rz_now / to_col(stat[0:1])
    parts = [a - alpha_0 * s for a, s in zip(parts, sums)]
    leaf_lanes = leaf_lanes - alpha_0 * of_line(1, 0)
    lanes = leaf_lanes + expand(own_coef(parts))
    leaf_prod = dots(of_line(0, 1) - alpha_0 * of_line(1, 1), leaf_lanes)

    product = apply_kernel(1, lanes, stats(leaf_prod))
    answer = alpha_0 * direction
    residual = rhs - alpha_0 * image
    leaf_res = leaf_res - alpha_0 * leaf_image
    precond = pick(lanes)
    leaf_total = to_col(product[cols : cols + 1])
    rz_next = leaf_total + level_product(parts)
    beta_0 = rz_next / rz_now
    rz_now = rz_next
    direction = precond + beta_0 * direction
    image = product[0:cols] + noise_level * precond + beta_0 * image
    leaf_image = leaf(image)
    put(2, image, (dots(direction, image), dots(image, leaf_res), dots(image, leaf_image)))
    reduce = by_subtree(2, cols + STATS)
    next(reduce)
    next(reduce)
    sums, stat = next(reduce)
    alpha_1 = rz_now / to_col(stat[0:1])
    sol_ref[...] = answer + alpha_1 * direction
    res_ref[...] = residual - alpha_1 * image
    parts = [a - alpha_1 * s for a, s in zip(parts, sums)]
    leaf_last = leaf_total - alpha_1 * (2.0 * to_col(stat[1:2]) - alpha_1 * to_col(stat[2:3]))
    beta_1 = (leaf_last + level_product(parts)) / rz_now
    for i, (alpha, beta) in enumerate(((alpha_0, beta_0), (alpha_1, beta_1))):
        coef_ref[0, i : i + 1, :] = to_row(alpha)[:, 0:cols]
        coef_ref[1, i : i + 1, :] = to_row(beta)[:, 0:cols]
    for at in range(3):
        length = long if at < 2 else cols + STATS
        all_line(line_ref.at[at, :, pl.ds(0, length)], 2 * at).wait_send()
        all_plane(plane_ref.at[at], 2 * at + 1).wait_send()
    for which in range(2):
        length = cols if which == 0 else cols + STATS
        all_plane(prod_ref.at[which, :, pl.ds(0, length)], 9 + which).wait_send()
    all_line(pts_line_ref, 6).wait_send()
    all_plane(pts_plane_ref, 7).wait_send()
    all_line(basis_ref, 8).wait_send()


def on_device(n_row, n_col, points, inverse_length, target, probe_bits, leaf_inverse, top_basis, sub_basis):
    low = math.gcd(n_col, 4)
    n_line, n_plane = low, n_row * (n_col // low)
    dim, own = points.shape
    cols = probe_bits.shape[0] + 1
    rank = top_basis.shape[0]
    vmem = pl.BlockSpec(memory_space=pltpu.VMEM)
    hbm = pl.BlockSpec(memory_space=pltpu.HBM)
    message = (cols + STATS, own)
    return pl.pallas_call(
        functools.partial(kernel, n_row, n_col, low, rank),
        out_shape=(
            jax.ShapeDtypeStruct((cols, own), F32),
            jax.ShapeDtypeStruct((cols, own), F32),
            jax.ShapeDtypeStruct((2, ITERS, cols), F32),
        ),
        in_specs=[hbm] * 7,
        out_specs=(vmem, vmem, vmem),
        scratch_shapes=[
            pltpu.VMEM(points.shape, F32),
            pltpu.VMEM((1, dim), F32),
            pltpu.VMEM(probe_bits.shape, jnp.int32),
            pltpu.VMEM(leaf_inverse.shape, F32),
            pltpu.VMEM((n_line, 2 * rank, own), F32),
            pltpu.VMEM((2 * rank, 2 * n_line * own), BF16),
            pltpu.VMEM((1, own), F32),
            pltpu.VMEM((cols, own), F32),
            pltpu.VMEM((n_line, dim, own), F32),
            pltpu.VMEM((n_plane, dim, own), F32),
            pltpu.VMEM((3, n_line, STATS + 3 * cols, own), F32),
            pltpu.VMEM((3, n_plane) + message, F32),
            pltpu.VMEM((2, n_plane) + message, F32),
            pltpu.VMEM((2 * (n_plane - 1),) + message, F32),
            pltpu.VMEM((n_plane // 2, n_line * own, 4 * own), BF16),
            pltpu.SemaphoreType.DMA((7,)),
            pltpu.SemaphoreType.DMA((11,)),
            pltpu.SemaphoreType.DMA((11,)),
        ],
        compiler_params=pltpu.CompilerParams(
            collective_id=0, has_side_effects=True, vmem_limit_bytes=62 * 1024 * 1024
        ),
    )(
        points,
        inverse_length.reshape(1, dim),
        target.reshape(1, own),
        probe_bits,
        leaf_inverse,
        top_basis,
        sub_basis,
    )


def solution(mesh):
    return jax.shard_map(
        functools.partial(on_device, mesh.shape["row"], mesh.shape["col"]),
        mesh=mesh,
        in_specs=(
            P(None, ("row", "col")),
            P(),
            P(("row", "col")),
            P(None, ("row", "col")),
            P(("row", "col"), None),
            P(None, ("row", "col")),
            P(None, ("row", "col")),
        ),
        out_specs=(P(None, ("row", "col")), P(None, ("row", "col")), P()),
        check_vma=False,
    )
```

```python
import functools
import math

import jax
import jax.numpy as jnp
from jax import lax
from jax.experimental import pallas as pl
from jax.experimental.pallas import tpu as pltpu
from jax.sharding import PartitionSpec as P

ITERS = 2
MESH = pl.DeviceIdType.MESH
F32 = jnp.float32
BF16 = jnp.bfloat16

root_five = math.sqrt(5.0)
noise_level = 0.5


def halves(x):
    hi = x.astype(BF16)
    return hi, (x - hi.astype(F32)).astype(BF16)


def thirds(x):
    hi = x.astype(BF16)
    rest = x - hi.astype(F32)
    mid = rest.astype(BF16)
    return hi, mid, (rest - mid.astype(F32)).astype(BF16)


def dot_nn(a, b):
    return lax.dot_general(a, b, (((1,), (0,)), ((), ())), preferred_element_type=F32)


def dot_nt(a, b):
    return lax.dot_general(a, b, (((1,), (1,)), ((), ())), preferred_element_type=F32)


def fold(out):
    rows, width = out.shape[0] // 2, out.shape[1] // 2
    return (
        (out[rows:, width:] + out[:rows, width:]) + out[rows:, :width]
    ) + out[:rows, :width]


def stacked(x):
    return jnp.concatenate(halves(x), axis=0)


def kernel(
    n_row,
    n_col,
    low,
    rank,
    points_hbm,
    length_hbm,
    target_hbm,
    bits_hbm,
    leaf_hbm,
    top_hbm,
    sub_hbm,
    sol_ref,
    res_ref,
    coef_ref,
    points_ref,
    length_ref,
    bits_ref,
    leaf_ref,
    basis_ref,
    wide_ref,
    target_ref,
    rhs_ref,
    pts_line_ref,
    pts_plane_ref,
    line_ref,
    line_stat_ref,
    extra_ref,
    plane_ref,
    plane_stat_ref,
    prod_ref,
    prod_stat_ref,
    out_ref,
    kmat_ref,
    load_sem,
    send_sem,
    recv_sem,
):
    n_high = n_col // low
    n_line, n_plane = low, n_row * n_high
    row, col = lax.axis_index("row"), lax.axis_index("col")
    high = lax.div(col, low)
    in_line = lax.rem(col, low)
    in_plane = row * n_high + high
    cols, own = rhs_ref.shape
    dim = points_ref.shape[0]

    line_peers = [(row, high * low + lax.rem(in_line + t, n_line)) for t in range(1, n_line)]
    plane_slots = [lax.rem(in_plane + t, n_plane) for t in range(n_plane)]
    plane_peers = [
        (lax.div(slot, n_high), lax.rem(slot, n_high) * low + in_line) for slot in plane_slots[1:]
    ]

    loads = [
        pltpu.make_async_copy(src, dst, load_sem.at[at])
        for at, (src, dst) in enumerate(
            (
                (points_hbm, points_ref),
                (length_hbm, length_ref),
                (target_hbm, target_ref),
                (bits_hbm, bits_ref),
                (top_hbm, basis_ref.at[in_line, pl.ds(0, rank)]),
                (sub_hbm, basis_ref.at[in_line, pl.ds(rank, rank)]),
                (leaf_hbm, leaf_ref),
            )
        )
    ]
    for load in loads:
        load.start()

    barrier = pltpu.get_barrier_semaphore()
    for peer in line_peers + plane_peers:
        pl.semaphore_signal(barrier, inc=1, device_id=peer, device_id_type=MESH)

    def remote(src, dst, at, device):
        return pltpu.make_async_remote_copy(
            src_ref=src,
            dst_ref=dst,
            send_sem=send_sem.at[at],
            recv_sem=recv_sem.at[at],
            device_id=device,
            device_id_type=MESH,
        )

    def send_line(buf, at):
        mine = buf.at[in_line]
        for peer in line_peers:
            remote(mine, mine, at, peer).start()

    def send_plane(buf, at):
        mine = buf.at[in_plane]
        for peer in plane_peers:
            remote(mine, mine, at, peer).start()

    def all_line(buf, at):
        some = buf.at[pl.ds(0, n_line - 1)]
        return remote(some, some, at, line_peers[0])

    def all_plane(buf, at):
        some = buf.at[pl.ds(0, n_plane - 1)]
        return remote(some, some, at, plane_peers[0])

    offset = lax.broadcasted_iota(jnp.int32, (cols, own), 1) - lax.broadcasted_iota(
        jnp.int32, (cols, own), 0
    )
    is_top = lax.broadcasted_iota(jnp.int32, (cols, 2 * rank), 1) < rank

    def to_row(*columns):
        spread = jnp.zeros((cols, own), F32)
        for at, column in enumerate(columns):
            spread = jnp.where(offset == at * cols, column, spread)
        return jnp.sum(spread, axis=0, keepdims=True)

    def to_col(line, at=0):
        return jnp.sum(jnp.where(offset == at * cols, line, 0.0), axis=1, keepdims=True)

    def dots(a, b):
        return jnp.sum(a * b, axis=1, keepdims=True)

    for load in loads[:4]:
        load.wait()
    rhs_ref[0:1, :] = target_ref[...]
    rhs_ref[1:cols, :] = 2.0 * bits_ref[...].astype(F32) - 1.0
    rhs = rhs_ref[...]
    inverse = jnp.sum(
        jnp.where(
            lax.broadcasted_iota(jnp.int32, (dim, dim), 0)
            == lax.broadcasted_iota(jnp.int32, (dim, dim), 1),
            length_ref[...],
            0.0,
        ),
        axis=1,
        keepdims=True,
    )
    scaled = points_ref[...] * inverse
    pts_line_ref[in_line] = scaled
    pts_plane_ref[in_plane] = scaled
    for load in loads[4:]:
        load.wait()
    basis_tall = stacked(basis_ref[in_line])
    leaf_tall = stacked(leaf_ref[...])

    def project(v):
        return fold(dot_nt(stacked(v), basis_tall))

    def expand(c):
        return fold(dot_nn(stacked(c), wide_ref[...]))

    def leaf(v):
        return fold(dot_nt(stacked(v), leaf_tall))

    def total(buf, first, count):
        out = buf[first]
        for i in range(first + 1, first + count):
            out = out + buf[i]
        return out

    def send_coef(at, vector):
        line_ref[at, in_line] = project(vector)
        send_line(line_ref.at[at], 4 * at)

    def send_stat(at, *columns):
        line_stat_ref[at, in_line] = to_row(*columns)
        send_line(line_stat_ref.at[at], 4 * at + 1)

    def send_extra(at, *more):
        for i, part in enumerate(more):
            extra_ref[at, in_line, i * cols : (i + 1) * cols, :] = part
        send_line(extra_ref.at[at], 12 + at)

    def cross(at):
        all_line(line_ref.at[at], 4 * at).wait_recv()
        plane_ref[at, in_plane] = total(line_ref.at[at], 0, n_line)
        send_plane(plane_ref.at[at], 4 * at + 2)
        all_line(line_stat_ref.at[at], 4 * at + 1).wait_recv()
        plane_stat_ref[at, in_plane] = total(line_stat_ref.at[at], 0, n_line)
        send_plane(plane_stat_ref.at[at], 4 * at + 3)

    def by_subtree(at):
        all_plane(plane_ref.at[at], 4 * at + 2).wait_recv()
        return [total(plane_ref.at[at], i * n_high, n_high) for i in range(n_row)]

    def all_stats(at):
        all_plane(plane_stat_ref.at[at], 4 * at + 3).wait_recv()
        return total(plane_stat_ref.at[at], 0, n_plane)

    def of_line(at, which):
        rows = slice(which * cols, (which + 1) * cols)
        return jnp.concatenate([extra_ref[at, i, rows, :] for i in range(n_line)], axis=1)

    def pick(lanes):
        mine = lanes[:, 0:own]
        for i in range(1, n_line):
            mine = jnp.where(in_line == i, lanes[:, i * own : (i + 1) * own], mine)
        return mine

    def own_coef(parts):
        mine = parts[0]
        for i in range(1, n_row):
            mine = jnp.where(row == i, parts[i], mine)
        return jnp.where(is_top, sum(parts[1:], parts[0]), mine)

    def level_product(parts):
        every = sum(parts[1:], parts[0])
        squares = jnp.where(is_top, every * every, 0.0)
        for part in parts:
            squares = squares + jnp.where(is_top, 0.0, part * part)
        return jnp.sum(squares, axis=1, keepdims=True)

    line_ref[0, in_line] = project(rhs)
    leaf_res = leaf(rhs)
    line_stat_ref[0, in_line] = to_row(dots(rhs, leaf_res))
    pl.semaphore_wait(barrier, n_line + n_plane - 2)
    send_line(line_ref.at[0], 0)
    send_line(line_stat_ref.at[0], 1)
    send_line(pts_line_ref, 14)
    send_plane(pts_plane_ref, 15)
    send_extra(0, leaf_res, rhs)
    send_line(basis_ref, 16)

    def norm_rows(sq, first):
        pieces = [p.astype(F32) for p in thirds(sq)]
        line = lax.broadcasted_iota(jnp.int32, (16, sq.shape[1]), 0)
        out = jnp.where((line >= 3 - 3 * first) & (line < 6 - 3 * first), 1.0, 0.0)
        for at, piece in enumerate(pieces):
            out = jnp.where(line == 3 * first + at, piece, out)
        return out.astype(BF16)

    def features(x, order, first):
        pieces = thirds(x)
        sq = jnp.sum(x * x, axis=0, keepdims=True)
        return [pieces[at] for at in order], norm_rows(sq, first)

    all_line(pts_line_ref, 14).wait_recv()
    sources = jnp.concatenate([pts_line_ref[i] for i in range(n_line)], axis=1)
    src_parts, src_norm = features(sources, (0, 0, 0, 1, 1, 2), 0)
    src_feat = jnp.concatenate(
        [-2.0 * p.astype(F32) for p in src_parts] + [src_norm.astype(F32)], axis=0
    ).T.astype(BF16)
    cross(0)
    all_plane(pts_plane_ref, 15).wait_recv()

    def build(q, carry):
        pair = jnp.concatenate(
            [pts_plane_ref[lax.rem(in_plane + 2 * q + i, n_plane)] for i in (1, 2)], axis=1
        )
        far_parts, far_norm = features(pair, (0, 1, 2, 0, 1, 0), 1)
        far_feat = jnp.concatenate(far_parts + [far_norm], axis=0)
        for i in range(n_line):
            some = src_feat[i * own : (i + 1) * own]
            five_sq = jnp.maximum(5.0 * dot_nn(some, far_feat), 1e-30)
            dist = five_sq * lax.rsqrt(five_sq)
            value = (1.0 + dist + five_sq * (1.0 / 3.0)) * jnp.exp(-dist)
            hi, lo = halves(value)
            kmat_ref[q, i * own : (i + 1) * own, 0 : 2 * own] = hi
            kmat_ref[q, i * own : (i + 1) * own, 2 * own :] = lo
        return carry

    lax.fori_loop(0, n_plane // 2, build, 0)

    all_line(basis_ref, 16).wait_recv()
    for i in range(n_line):
        hi, lo = halves(basis_ref[i])
        wide_ref[:, i * own : (i + 1) * own] = hi
        wide_ref[:, (n_line + i) * own : (n_line + i + 1) * own] = lo

    def send_products(which, vectors):
        mine = stacked(vectors)
        for q in range(n_plane // 2):
            both = fold(dot_nn(mine, kmat_ref[q]))
            for half in range(2):
                t = 2 * q + 1 + half
                block = both[:, half * own : (half + 1) * own]
                if t == n_plane:
                    prod_ref[which, in_plane] = block
                    continue
                slot = which * (n_plane - 1) + t - 1
                out_ref[slot] = block
                remote(
                    out_ref.at[slot], prod_ref.at[which, in_plane], 17 + which, plane_peers[t - 1]
                ).start()

    def products(which):
        all_plane(prod_ref.at[which], 17 + which).wait_recv()
        return total(prod_ref.at[which], 0, n_plane)

    all_line(extra_ref.at[0], 12).wait_recv()
    leaf_lanes = of_line(0, 0)
    parts = by_subtree(0)
    lanes = leaf_lanes + expand(own_coef(parts))
    send_products(0, lanes)
    direction = pick(lanes)
    rz_now = to_col(all_stats(0)) + level_product(parts)

    image = products(0) + noise_level * direction
    send_coef(1, image)
    send_stat(1, dots(direction, image))
    leaf_image = leaf(image)
    send_extra(1, leaf_image, image)
    cross(1)
    all_line(extra_ref.at[1], 13).wait_recv()
    leaf_step = of_line(1, 0)
    alpha_0 = rz_now / to_col(all_stats(1))
    sums = by_subtree(1)
    parts = [a - alpha_0 * s for a, s in zip(parts, sums)]
    leaf_lanes = leaf_lanes - alpha_0 * leaf_step
    lanes = leaf_lanes + expand(own_coef(parts))
    send_products(1, lanes)
    residual_lanes = of_line(0, 1) - alpha_0 * of_line(1, 1)
    prod_stat_ref[in_plane] = to_row(dots(residual_lanes, leaf_lanes))
    send_plane(prod_stat_ref, 19)
    answer = alpha_0 * direction
    residual = rhs - alpha_0 * image
    leaf_res = leaf_res - alpha_0 * leaf_image
    precond = pick(lanes)
    levels = level_product(parts)

    all_plane(prod_stat_ref, 19).wait_recv()
    leaf_total = to_col(total(prod_stat_ref, 0, n_plane))
    rz_next = leaf_total + levels
    beta_0 = rz_next / rz_now
    rz_now = rz_next
    direction = precond + beta_0 * direction
    rest = noise_level * precond + beta_0 * image
    image = products(1) + rest
    send_coef(2, image)
    leaf_image = leaf(image)
    send_stat(2, dots(direction, image), dots(image, leaf_res), dots(image, leaf_image))
    cross(2)
    stat = all_stats(2)
    alpha_1 = rz_now / to_col(stat)
    sol_ref[...] = answer + alpha_1 * direction
    res_ref[...] = residual - alpha_1 * image
    leaf_last = leaf_total - alpha_1 * (2.0 * to_col(stat, 1) - alpha_1 * to_col(stat, 2))
    parts = [a - alpha_1 * s for a, s in zip(parts, by_subtree(2))]
    beta_1 = (leaf_last + level_product(parts)) / rz_now
    for i, (alpha, beta) in enumerate(((alpha_0, beta_0), (alpha_1, beta_1))):
        coef_ref[0, i : i + 1, :] = to_row(alpha)[:, 0:cols]
        coef_ref[1, i : i + 1, :] = to_row(beta)[:, 0:cols]
    for at in range(3):
        all_line(line_ref.at[at], 4 * at).wait_send()
        all_line(line_stat_ref.at[at], 4 * at + 1).wait_send()
        all_plane(plane_ref.at[at], 4 * at + 2).wait_send()
        all_plane(plane_stat_ref.at[at], 4 * at + 3).wait_send()
    for at in range(2):
        all_line(extra_ref.at[at], 12 + at).wait_send()
        all_plane(prod_ref.at[at], 17 + at).wait_send()
    all_line(pts_line_ref, 14).wait_send()
    all_plane(pts_plane_ref, 15).wait_send()
    all_line(basis_ref, 16).wait_send()
    all_plane(prod_stat_ref, 19).wait_send()


def on_device(n_row, n_col, points, inverse_length, target, probe_bits, leaf_inverse, top_basis, sub_basis):
    low = math.gcd(n_col, 4)
    n_line, n_plane = low, n_row * (n_col // low)
    dim, own = points.shape
    cols = probe_bits.shape[0] + 1
    rank = top_basis.shape[0]
    vmem = pl.BlockSpec(memory_space=pltpu.VMEM)
    hbm = pl.BlockSpec(memory_space=pltpu.HBM)
    message = (cols, own)
    return pl.pallas_call(
        functools.partial(kernel, n_row, n_col, low, rank),
        out_shape=(
            jax.ShapeDtypeStruct((cols, own), F32),
            jax.ShapeDtypeStruct((cols, own), F32),
            jax.ShapeDtypeStruct((2, ITERS, cols), F32),
        ),
        in_specs=[hbm] * 7,
        out_specs=(vmem, vmem, vmem),
        scratch_shapes=[
            pltpu.VMEM(points.shape, F32),
            pltpu.VMEM((1, dim), F32),
            pltpu.VMEM(probe_bits.shape, jnp.int32),
            pltpu.VMEM(leaf_inverse.shape, F32),
            pltpu.VMEM((n_line, 2 * rank, own), F32),
            pltpu.VMEM((2 * rank, 2 * n_line * own), BF16),
            pltpu.VMEM((1, own), F32),
            pltpu.VMEM((cols, own), F32),
            pltpu.VMEM((n_line, dim, own), F32),
            pltpu.VMEM((n_plane, dim, own), F32),
            pltpu.VMEM((3, n_line) + message, F32),
            pltpu.VMEM((3, n_line, 1, own), F32),
            pltpu.VMEM((2, n_line, 2 * cols, own), F32),
            pltpu.VMEM((3, n_plane) + message, F32),
            pltpu.VMEM((3, n_plane, 1, own), F32),
            pltpu.VMEM((2, n_plane) + message, F32),
            pltpu.VMEM((n_plane, 1, own), F32),
            pltpu.VMEM((2 * (n_plane - 1),) + message, F32),
            pltpu.VMEM((n_plane // 2, n_line * own, 4 * own), BF16),
            pltpu.SemaphoreType.DMA((7,)),
            pltpu.SemaphoreType.DMA((20,)),
            pltpu.SemaphoreType.DMA((20,)),
        ],
        compiler_params=pltpu.CompilerParams(
            collective_id=0, has_side_effects=True, vmem_limit_bytes=62 * 1024 * 1024
        ),
    )(
        points,
        inverse_length.reshape(1, dim),
        target.reshape(1, own),
        probe_bits,
        leaf_inverse,
        top_basis,
        sub_basis,
    )


def solution(mesh):
    return jax.shard_map(
        functools.partial(on_device, mesh.shape["row"], mesh.shape["col"]),
        mesh=mesh,
        in_specs=(
            P(None, ("row", "col")),
            P(),
            P(("row", "col")),
            P(None, ("row", "col")),
            P(("row", "col"), None),
            P(None, ("row", "col")),
            P(None, ("row", "col")),
        ),
        out_specs=(P(None, ("row", "col")), P(None, ("row", "col")), P()),
        check_vma=False,
    )
```

```python
import functools
import math

import jax
import jax.numpy as jnp
from jax import lax
from jax.experimental import pallas as pl
from jax.experimental.pallas import tpu as pltpu
from jax.sharding import PartitionSpec as P

ITERS = 2
MESH = pl.DeviceIdType.MESH
F32 = jnp.float32
BF16 = jnp.bfloat16

root_five = math.sqrt(5.0)
noise_level = 0.5


def halves(x):
    hi = x.astype(BF16)
    return hi, (x - hi.astype(F32)).astype(BF16)


def thirds(x):
    hi = x.astype(BF16)
    rest = x - hi.astype(F32)
    mid = rest.astype(BF16)
    return hi, mid, (rest - mid.astype(F32)).astype(BF16)


def dot_nn(a, b):
    return lax.dot_general(a, b, (((1,), (0,)), ((), ())), preferred_element_type=F32)


def fold(out):
    rows, width = out.shape[0] // 2, out.shape[1] // 2
    return (
        (out[rows:, width:] + out[:rows, width:]) + out[rows:, :width]
    ) + out[:rows, :width]


def stacked(x):
    return jnp.concatenate(halves(x), axis=0)


def beside(x):
    return jnp.concatenate(halves(x), axis=1)


def kernel(
    n_row,
    n_col,
    low,
    rank,
    points_hbm,
    length_hbm,
    target_hbm,
    bits_hbm,
    leaf_hbm,
    top_hbm,
    sub_hbm,
    sol_ref,
    res_ref,
    coef_ref,
    points_ref,
    length_ref,
    bits_ref,
    leaf_ref,
    basis_ref,
    wide_ref,
    target_ref,
    rhs_ref,
    pts_line_ref,
    pts_plane_ref,
    line_ref,
    line_stat_ref,
    extra_ref,
    plane_ref,
    plane_stat_ref,
    prod_ref,
    prod_stat_ref,
    out_ref,
    kmat_ref,
    load_sem,
    send_sem,
    recv_sem,
):
    n_high = n_col // low
    n_line, n_plane = n_high, n_row * low
    row, col = lax.axis_index("row"), lax.axis_index("col")
    high = lax.div(col, low)
    lowest = lax.rem(col, low)
    in_line = high
    in_plane = row * low + lowest
    cols, own = rhs_ref.shape
    dim = points_ref.shape[0]

    line_peers = [(row, lax.rem(in_line + t, n_line) * low + lowest) for t in range(1, n_line)]
    plane_slots = [lax.rem(in_plane + t, n_plane) for t in range(n_plane)]
    plane_peers = [
        (lax.div(slot, low), in_line * low + lax.rem(slot, low)) for slot in plane_slots[1:]
    ]

    loads = [
        pltpu.make_async_copy(src, dst, load_sem.at[at])
        for at, (src, dst) in enumerate(
            (
                (points_hbm, points_ref),
                (length_hbm, length_ref),
                (target_hbm, target_ref),
                (bits_hbm, bits_ref),
                (top_hbm, basis_ref.at[in_line, pl.ds(0, rank)]),
                (sub_hbm, basis_ref.at[in_line, pl.ds(rank, rank)]),
                (leaf_hbm, leaf_ref),
            )
        )
    ]
    for load in loads:
        load.start()

    barrier = pltpu.get_barrier_semaphore()
    for peer in line_peers + plane_peers:
        pl.semaphore_signal(barrier, inc=1, device_id=peer, device_id_type=MESH)

    def remote(src, dst, at, device):
        return pltpu.make_async_remote_copy(
            src_ref=src,
            dst_ref=dst,
            send_sem=send_sem.at[at],
            recv_sem=recv_sem.at[at],
            device_id=device,
            device_id_type=MESH,
        )

    def send_line(buf, at):
        mine = buf.at[in_line]
        for peer in line_peers:
            remote(mine, mine, at, peer).start()

    def send_plane(buf, at):
        mine = buf.at[in_plane]
        for peer in plane_peers:
            remote(mine, mine, at, peer).start()

    def all_line(buf, at):
        some = buf.at[pl.ds(0, n_line - 1)]
        return remote(some, some, at, line_peers[0])

    def all_plane(buf, at):
        some = buf.at[pl.ds(0, n_plane - 1)]
        return remote(some, some, at, plane_peers[0])

    offset = lax.broadcasted_iota(jnp.int32, (cols, own), 1) - lax.broadcasted_iota(
        jnp.int32, (cols, own), 0
    )
    is_top = lax.broadcasted_iota(jnp.int32, (cols, 2 * rank), 1) < rank

    def to_row(*columns):
        spread = jnp.zeros((cols, own), F32)
        for at, column in enumerate(columns):
            spread = jnp.where(offset == at * cols, column, spread)
        return jnp.sum(spread, axis=0, keepdims=True)

    def to_col(line, at=0):
        return jnp.sum(jnp.where(offset == at * cols, line, 0.0), axis=1, keepdims=True)

    def dots(a, b):
        return jnp.sum(a * b, axis=1, keepdims=True)

    for load in loads[:4]:
        load.wait()
    rhs_ref[0:1, :] = target_ref[...]
    rhs_ref[1:cols, :] = 2.0 * bits_ref[...].astype(F32) - 1.0
    rhs = rhs_ref[...]
    inverse = jnp.sum(
        jnp.where(
            lax.broadcasted_iota(jnp.int32, (dim, dim), 0)
            == lax.broadcasted_iota(jnp.int32, (dim, dim), 1),
            length_ref[...],
            0.0,
        ),
        axis=1,
        keepdims=True,
    )
    scaled = points_ref[...] * inverse
    pts_line_ref[in_line] = scaled
    pts_plane_ref[in_plane] = scaled
    for load in loads[4:]:
        load.wait()
    basis_wide = beside(basis_ref[in_line].T)
    leaf_wide = beside(leaf_ref[...])

    def project(v):
        return fold(dot_nn(stacked(v), basis_wide))

    def expand(c):
        return fold(dot_nn(stacked(c), wide_ref[...]))

    def leaf(v):
        return fold(dot_nn(stacked(v), leaf_wide))

    def total(buf, first, count):
        out = buf[first]
        for i in range(first + 1, first + count):
            out = out + buf[i]
        return out

    def send_coef(at, vector):
        line_ref[at, in_line] = project(vector)
        send_line(line_ref.at[at], 4 * at)

    def send_stat(at, *columns):
        line_stat_ref[at, in_line] = to_row(*columns)
        send_line(line_stat_ref.at[at], 4 * at + 1)

    def send_extra(at, *more):
        for i, part in enumerate(more):
            extra_ref[at, in_line, i * cols : (i + 1) * cols, :] = part
        send_line(extra_ref.at[at], 12 + at)

    def cross(at):
        all_line(line_ref.at[at], 4 * at).wait_recv()
        plane_ref[at, in_plane] = total(line_ref.at[at], 0, n_line)
        send_plane(plane_ref.at[at], 4 * at + 2)
        all_line(line_stat_ref.at[at], 4 * at + 1).wait_recv()
        plane_stat_ref[at, in_plane] = total(line_stat_ref.at[at], 0, n_line)
        send_plane(plane_stat_ref.at[at], 4 * at + 3)

    def by_subtree(at):
        all_plane(plane_ref.at[at], 4 * at + 2).wait_recv()
        return [total(plane_ref.at[at], i * low, low) for i in range(n_row)]

    def all_stats(at):
        all_plane(plane_stat_ref.at[at], 4 * at + 3).wait_recv()
        return total(plane_stat_ref.at[at], 0, n_plane)

    def of_line(at, which):
        rows = slice(which * cols, (which + 1) * cols)
        return jnp.concatenate([extra_ref[at, i, rows, :] for i in range(n_line)], axis=1)

    def pick(lanes):
        mine = lanes[:, 0:own]
        for i in range(1, n_line):
            mine = jnp.where(in_line == i, lanes[:, i * own : (i + 1) * own], mine)
        return mine

    def own_coef(parts):
        mine = parts[0]
        for i in range(1, n_row):
            mine = jnp.where(row == i, parts[i], mine)
        return jnp.where(is_top, sum(parts[1:], parts[0]), mine)

    def level_product(parts):
        every = sum(parts[1:], parts[0])
        squares = jnp.where(is_top, every * every, 0.0)
        for part in parts:
            squares = squares + jnp.where(is_top, 0.0, part * part)
        return jnp.sum(squares, axis=1, keepdims=True)

    line_ref[0, in_line] = project(rhs)
    leaf_res = leaf(rhs)
    line_stat_ref[0, in_line] = to_row(dots(rhs, leaf_res))
    pl.semaphore_wait(barrier, n_line + n_plane - 2)
    send_line(line_ref.at[0], 0)
    send_line(line_stat_ref.at[0], 1)
    send_line(pts_line_ref, 14)
    send_plane(pts_plane_ref, 15)
    send_extra(0, leaf_res, rhs)
    send_line(basis_ref, 16)

    def norm_rows(sq, first):
        pieces = [p.astype(F32) for p in thirds(sq)]
        line = lax.broadcasted_iota(jnp.int32, (16, sq.shape[1]), 0)
        out = jnp.where((line >= 3 - 3 * first) & (line < 6 - 3 * first), 1.0, 0.0)
        for at, piece in enumerate(pieces):
            out = jnp.where(line == 3 * first + at, piece, out)
        return out.astype(BF16)

    def features(x, order, first):
        pieces = thirds(x)
        sq = jnp.sum(x * x, axis=0, keepdims=True)
        return [pieces[at] for at in order], norm_rows(sq, first)

    all_line(pts_line_ref, 14).wait_recv()
    sources = jnp.concatenate([pts_line_ref[i] for i in range(n_line)], axis=1)
    src_parts, src_norm = features(sources, (0, 0, 0, 1, 1, 2), 0)
    src_feat = jnp.concatenate(
        [-2.0 * p.astype(F32) for p in src_parts] + [src_norm.astype(F32)], axis=0
    ).T.astype(BF16)
    cross(0)
    all_plane(pts_plane_ref, 15).wait_recv()

    def build(q, carry):
        pair = jnp.concatenate(
            [pts_plane_ref[lax.rem(in_plane + 2 * q + i, n_plane)] for i in (1, 2)], axis=1
        )
        far_parts, far_norm = features(pair, (0, 1, 2, 0, 1, 0), 1)
        far_feat = jnp.concatenate(far_parts + [far_norm], axis=0)
        for i in range(n_line):
            some = src_feat[i * own : (i + 1) * own]
            five_sq = jnp.maximum(5.0 * dot_nn(some, far_feat), 1e-30)
            dist = five_sq * lax.rsqrt(five_sq)
            value = (1.0 + dist + five_sq * (1.0 / 3.0)) * jnp.exp(-dist)
            hi, lo = halves(value)
            kmat_ref[q, i * own : (i + 1) * own, 0 : 2 * own] = hi
            kmat_ref[q, i * own : (i + 1) * own, 2 * own :] = lo
        return carry

    lax.fori_loop(0, n_plane // 2, build, 0)

    all_line(basis_ref, 16).wait_recv()
    for i in range(n_line):
        hi, lo = halves(basis_ref[i])
        wide_ref[:, i * own : (i + 1) * own] = hi
        wide_ref[:, (n_line + i) * own : (n_line + i + 1) * own] = lo

    def send_products(which, vectors):
        mine = stacked(vectors)
        for q in range(n_plane // 2):
            both = fold(dot_nn(mine, kmat_ref[q]))
            for half in range(2):
                t = 2 * q + 1 + half
                block = both[:, half * own : (half + 1) * own]
                if t == n_plane:
                    prod_ref[which, in_plane] = block
                    continue
                slot = which * (n_plane - 1) + t - 1
                out_ref[slot] = block
                remote(
                    out_ref.at[slot], prod_ref.at[which, in_plane], 17 + which, plane_peers[t - 1]
                ).start()

    def products(which):
        all_plane(prod_ref.at[which], 17 + which).wait_recv()
        return total(prod_ref.at[which], 0, n_plane)

    all_line(extra_ref.at[0], 12).wait_recv()
    leaf_lanes = of_line(0, 0)
    parts = by_subtree(0)
    lanes = leaf_lanes + expand(own_coef(parts))
    send_products(0, lanes)
    direction = pick(lanes)
    rz_now = to_col(all_stats(0)) + level_product(parts)

    image = products(0) + noise_level * direction
    send_coef(1, image)
    send_stat(1, dots(direction, image))
    leaf_image = leaf(image)
    send_extra(1, leaf_image, image)
    cross(1)
    all_line(extra_ref.at[1], 13).wait_recv()
    leaf_step = of_line(1, 0)
    alpha_0 = rz_now / to_col(all_stats(1))
    sums = by_subtree(1)
    parts = [a - alpha_0 * s for a, s in zip(parts, sums)]
    leaf_lanes = leaf_lanes - alpha_0 * leaf_step
    lanes = leaf_lanes + expand(own_coef(parts))
    send_products(1, lanes)
    residual_lanes = of_line(0, 1) - alpha_0 * of_line(1, 1)
    prod_stat_ref[in_plane] = to_row(dots(residual_lanes, leaf_lanes))
    send_plane(prod_stat_ref, 19)
    answer = alpha_0 * direction
    residual = rhs - alpha_0 * image
    leaf_res = leaf_res - alpha_0 * leaf_image
    precond = pick(lanes)
    levels = level_product(parts)

    all_plane(prod_stat_ref, 19).wait_recv()
    leaf_total = to_col(total(prod_stat_ref, 0, n_plane))
    rz_next = leaf_total + levels
    beta_0 = rz_next / rz_now
    rz_now = rz_next
    direction = precond + beta_0 * direction
    rest = noise_level * precond + beta_0 * image
    image = products(1) + rest
    send_coef(2, image)
    leaf_image = leaf(image)
    send_stat(2, dots(direction, image), dots(image, leaf_res), dots(image, leaf_image))
    cross(2)
    stat = all_stats(2)
    alpha_1 = rz_now / to_col(stat)
    sol_ref[...] = answer + alpha_1 * direction
    res_ref[...] = residual - alpha_1 * image
    leaf_last = leaf_total - alpha_1 * (2.0 * to_col(stat, 1) - alpha_1 * to_col(stat, 2))
    parts = [a - alpha_1 * s for a, s in zip(parts, by_subtree(2))]
    beta_1 = (leaf_last + level_product(parts)) / rz_now
    for i, (alpha, beta) in enumerate(((alpha_0, beta_0), (alpha_1, beta_1))):
        coef_ref[0, i : i + 1, :] = to_row(alpha)[:, 0:cols]
        coef_ref[1, i : i + 1, :] = to_row(beta)[:, 0:cols]
    for at in range(3):
        all_line(line_ref.at[at], 4 * at).wait_send()
        all_line(line_stat_ref.at[at], 4 * at + 1).wait_send()
        all_plane(plane_ref.at[at], 4 * at + 2).wait_send()
        all_plane(plane_stat_ref.at[at], 4 * at + 3).wait_send()
    for at in range(2):
        all_line(extra_ref.at[at], 12 + at).wait_send()
        all_plane(prod_ref.at[at], 17 + at).wait_send()
    all_line(pts_line_ref, 14).wait_send()
    all_plane(pts_plane_ref, 15).wait_send()
    all_line(basis_ref, 16).wait_send()
    all_plane(prod_stat_ref, 19).wait_send()


def on_device(n_row, n_col, points, inverse_length, target, probe_bits, leaf_inverse, top_basis, sub_basis):
    low = math.gcd(n_col, 4)
    n_line, n_plane = n_col // low, n_row * low
    dim, own = points.shape
    cols = probe_bits.shape[0] + 1
    rank = top_basis.shape[0]
    vmem = pl.BlockSpec(memory_space=pltpu.VMEM)
    hbm = pl.BlockSpec(memory_space=pltpu.HBM)
    message = (cols, own)
    return pl.pallas_call(
        functools.partial(kernel, n_row, n_col, low, rank),
        out_shape=(
            jax.ShapeDtypeStruct((cols, own), F32),
            jax.ShapeDtypeStruct((cols, own), F32),
            jax.ShapeDtypeStruct((2, ITERS, cols), F32),
        ),
        in_specs=[hbm] * 7,
        out_specs=(vmem, vmem, vmem),
        scratch_shapes=[
            pltpu.VMEM(points.shape, F32),
            pltpu.VMEM((1, dim), F32),
            pltpu.VMEM(probe_bits.shape, jnp.int32),
            pltpu.VMEM(leaf_inverse.shape, F32),
            pltpu.VMEM((n_line, 2 * rank, own), F32),
            pltpu.VMEM((2 * rank, 2 * n_line * own), BF16),
            pltpu.VMEM((1, own), F32),
            pltpu.VMEM((cols, own), F32),
            pltpu.VMEM((n_line, dim, own), F32),
            pltpu.VMEM((n_plane, dim, own), F32),
            pltpu.VMEM((3, n_line) + message, F32),
            pltpu.VMEM((3, n_line, 1, own), F32),
            pltpu.VMEM((2, n_line, 2 * cols, own), F32),
            pltpu.VMEM((3, n_plane) + message, F32),
            pltpu.VMEM((3, n_plane, 1, own), F32),
            pltpu.VMEM((2, n_plane) + message, F32),
            pltpu.VMEM((n_plane, 1, own), F32),
            pltpu.VMEM((2 * (n_plane - 1),) + message, F32),
            pltpu.VMEM((n_plane // 2, n_line * own, 4 * own), BF16),
            pltpu.SemaphoreType.DMA((7,)),
            pltpu.SemaphoreType.DMA((20,)),
            pltpu.SemaphoreType.DMA((20,)),
        ],
        compiler_params=pltpu.CompilerParams(
            collective_id=0, has_side_effects=True, vmem_limit_bytes=62 * 1024 * 1024
        ),
    )(
        points,
        inverse_length.reshape(1, dim),
        target.reshape(1, own),
        probe_bits,
        leaf_inverse,
        top_basis,
        sub_basis,
    )


def solution(mesh):
    return jax.shard_map(
        functools.partial(on_device, mesh.shape["row"], mesh.shape["col"]),
        mesh=mesh,
        in_specs=(
            P(None, ("row", "col")),
            P(),
            P(("row", "col")),
            P(None, ("row", "col")),
            P(("row", "col"), None),
            P(None, ("row", "col")),
            P(None, ("row", "col")),
        ),
        out_specs=(P(None, ("row", "col")), P(None, ("row", "col")), P()),
        check_vma=False,
    )
```

```python
import functools
import math

import jax
import jax.numpy as jnp
from jax import lax
from jax.experimental import pallas as pl
from jax.experimental.pallas import tpu as pltpu
from jax.sharding import PartitionSpec as P

ITERS = 2
MESH = pl.DeviceIdType.MESH
F32 = jnp.float32
BF16 = jnp.bfloat16

root_five = math.sqrt(5.0)
noise_level = 0.5


def halves(x):
    hi = x.astype(BF16)
    return hi, (x - hi.astype(F32)).astype(BF16)


def thirds(x):
    hi = x.astype(BF16)
    rest = x - hi.astype(F32)
    mid = rest.astype(BF16)
    return hi, mid, (rest - mid.astype(F32)).astype(BF16)


def dot_nn(a, b):
    return lax.dot_general(a, b, (((1,), (0,)), ((), ())), preferred_element_type=F32)


def fold(out):
    rows, width = out.shape[0] // 2, out.shape[1] // 2
    return (
        (out[rows:, width:] + out[:rows, width:]) + out[rows:, :width]
    ) + out[:rows, :width]


def stacked(x):
    return jnp.concatenate(halves(x), axis=0)


def beside(x):
    return jnp.concatenate(halves(x), axis=1)


def kernel(
    n_row,
    n_col,
    low,
    rank,
    points_hbm,
    length_hbm,
    target_hbm,
    bits_hbm,
    leaf_hbm,
    top_hbm,
    sub_hbm,
    sol_ref,
    res_ref,
    coef_ref,
    points_ref,
    length_ref,
    bits_ref,
    leaf_ref,
    basis_ref,
    wide_ref,
    target_ref,
    rhs_ref,
    pts_line_ref,
    pts_plane_ref,
    line_ref,
    extra_ref,
    plane_ref,
    prod_ref,
    prod_stat_ref,
    out_ref,
    out_stat_ref,
    kmat_ref,
    load_sem,
    send_sem,
    recv_sem,
):
    n_high = n_col // low
    n_line, n_plane = low, n_row * n_high
    row, col = lax.axis_index("row"), lax.axis_index("col")
    high = lax.div(col, low)
    in_line = lax.rem(col, low)
    in_plane = row * n_high + high
    cols, own = rhs_ref.shape
    dim = points_ref.shape[0]

    line_peers = [(row, high * low + lax.rem(in_line + t, n_line)) for t in range(1, n_line)]
    plane_slots = [lax.rem(in_plane + t, n_plane) for t in range(n_plane)]
    plane_peers = [
        (lax.div(slot, n_high), lax.rem(slot, n_high) * low + in_line) for slot in plane_slots[1:]
    ]

    loads = [
        pltpu.make_async_copy(src, dst, load_sem.at[at])
        for at, (src, dst) in enumerate(
            (
                (points_hbm, points_ref),
                (length_hbm, length_ref),
                (target_hbm, target_ref),
                (bits_hbm, bits_ref),
                (top_hbm, basis_ref.at[in_line, pl.ds(0, rank)]),
                (sub_hbm, basis_ref.at[in_line, pl.ds(rank, rank)]),
                (leaf_hbm, leaf_ref),
            )
        )
    ]
    for load in loads:
        load.start()

    barrier = pltpu.get_barrier_semaphore()
    for peer in line_peers + plane_peers:
        pl.semaphore_signal(barrier, inc=1, device_id=peer, device_id_type=MESH)

    def remote(src, dst, at, device):
        return pltpu.make_async_remote_copy(
            src_ref=src,
            dst_ref=dst,
            send_sem=send_sem.at[at],
            recv_sem=recv_sem.at[at],
            device_id=device,
            device_id_type=MESH,
        )

    def send_line(buf, at):
        mine = buf.at[in_line]
        for peer in line_peers:
            remote(mine, mine, at, peer).start()

    def send_plane(buf, at):
        mine = buf.at[in_plane]
        for peer in plane_peers:
            remote(mine, mine, at, peer).start()

    def all_line(buf, at):
        some = buf.at[pl.ds(0, n_line - 1)]
        return remote(some, some, at, line_peers[0])

    def all_plane(buf, at):
        some = buf.at[pl.ds(0, n_plane - 1)]
        return remote(some, some, at, plane_peers[0])

    offset = lax.broadcasted_iota(jnp.int32, (cols, own), 1) - lax.broadcasted_iota(
        jnp.int32, (cols, own), 0
    )
    is_top = lax.broadcasted_iota(jnp.int32, (cols, 2 * rank), 1) < rank

    def to_row(*columns):
        spread = jnp.zeros((cols, own), F32)
        for at, column in enumerate(columns):
            spread = jnp.where(offset == at * cols, column, spread)
        return jnp.sum(spread, axis=0, keepdims=True)

    def to_col(line, at=0):
        return jnp.sum(jnp.where(offset == at * cols, line, 0.0), axis=1, keepdims=True)

    def dots(a, b):
        return jnp.sum(a * b, axis=1, keepdims=True)

    for load in loads[:4]:
        load.wait()
    rhs_ref[0:1, :] = target_ref[...]
    rhs_ref[1:cols, :] = 2.0 * bits_ref[...].astype(F32) - 1.0
    rhs = rhs_ref[...]
    inverse = jnp.sum(
        jnp.where(
            lax.broadcasted_iota(jnp.int32, (dim, dim), 0)
            == lax.broadcasted_iota(jnp.int32, (dim, dim), 1),
            length_ref[...],
            0.0,
        ),
        axis=1,
        keepdims=True,
    )
    scaled = points_ref[...] * inverse
    pts_line_ref[in_line] = scaled
    pts_plane_ref[in_plane] = scaled
    for load in loads[4:]:
        load.wait()
    basis_wide = beside(basis_ref[in_line].T)
    leaf_wide = beside(leaf_ref[...])

    def project(v):
        return fold(dot_nn(stacked(v), basis_wide))

    def expand(c):
        return fold(dot_nn(stacked(c), wide_ref[...]))

    def leaf(v):
        return fold(dot_nn(stacked(v), leaf_wide))

    def total(buf, first, count):
        out = buf[first]
        for i in range(first + 1, first + count):
            out = out + buf[i]
        return out

    def put(at, vector, *columns):
        line_ref[at, in_line, 0:cols, :] = project(vector)
        line_ref[at, in_line, cols : cols + 1, :] = to_row(*columns)

    def send_extra(at, *more):
        for i, part in enumerate(more):
            extra_ref[at, in_line, i * cols : (i + 1) * cols, :] = part
        send_line(extra_ref.at[at], 6 + at)

    def cross(at):
        all_line(line_ref.at[at], at).wait_recv()
        plane_ref[at, in_plane] = total(line_ref.at[at], 0, n_line)
        send_plane(plane_ref.at[at], 3 + at)

    def by_subtree(at):
        all_plane(plane_ref.at[at], 3 + at).wait_recv()
        sums = [total(plane_ref.at[at], i * n_high, n_high) for i in range(n_row)]
        return [s[0:cols] for s in sums], sum([s[cols:] for s in sums[1:]], sums[0][cols:])

    def of_line(at, which):
        rows = slice(which * cols, (which + 1) * cols)
        return jnp.concatenate([extra_ref[at, i, rows, :] for i in range(n_line)], axis=1)

    def pick(lanes):
        mine = lanes[:, 0:own]
        for i in range(1, n_line):
            mine = jnp.where(in_line == i, lanes[:, i * own : (i + 1) * own], mine)
        return mine

    def own_coef(parts):
        mine = parts[0]
        for i in range(1, n_row):
            mine = jnp.where(row == i, parts[i], mine)
        return jnp.where(is_top, sum(parts[1:], parts[0]), mine)

    def level_product(parts):
        every = sum(parts[1:], parts[0])
        squares = jnp.where(is_top, every * every, 0.0)
        for part in parts:
            squares = squares + jnp.where(is_top, 0.0, part * part)
        return jnp.sum(squares, axis=1, keepdims=True)

    leaf_res = leaf(rhs)
    put(0, rhs, dots(rhs, leaf_res))
    pl.semaphore_wait(barrier, n_line + n_plane - 2)
    send_line(line_ref.at[0], 0)
    send_line(pts_line_ref, 8)
    send_plane(pts_plane_ref, 9)
    send_extra(0, leaf_res, rhs)
    send_line(basis_ref, 10)

    def norm_rows(sq, first):
        pieces = [p.astype(F32) for p in thirds(sq)]
        line = lax.broadcasted_iota(jnp.int32, (16, sq.shape[1]), 0)
        out = jnp.where((line >= 3 - 3 * first) & (line < 6 - 3 * first), 1.0, 0.0)
        for at, piece in enumerate(pieces):
            out = jnp.where(line == 3 * first + at, piece, out)
        return out.astype(BF16)

    def features(x, order, first):
        pieces = thirds(x)
        sq = jnp.sum(x * x, axis=0, keepdims=True)
        return [pieces[at] for at in order], norm_rows(sq, first)

    all_line(pts_line_ref, 8).wait_recv()
    sources = jnp.concatenate([pts_line_ref[i] for i in range(n_line)], axis=1)
    src_parts, src_norm = features(sources, (0, 0, 0, 1, 1, 2), 0)
    src_feat = jnp.concatenate(
        [-2.0 * p.astype(F32) for p in src_parts] + [src_norm.astype(F32)], axis=0
    ).T.astype(BF16)
    cross(0)
    all_plane(pts_plane_ref, 9).wait_recv()

    def build(q, carry):
        pair = jnp.concatenate(
            [pts_plane_ref[lax.rem(in_plane + 2 * q + i, n_plane)] for i in (1, 2)], axis=1
        )
        far_parts, far_norm = features(pair, (0, 1, 2, 0, 1, 0), 1)
        far_feat = jnp.concatenate(far_parts + [far_norm], axis=0)
        for i in range(n_line):
            some = src_feat[i * own : (i + 1) * own]
            five_sq = jnp.maximum(5.0 * dot_nn(some, far_feat), 1e-30)
            dist = five_sq * lax.rsqrt(five_sq)
            value = (1.0 + dist + five_sq * (1.0 / 3.0)) * jnp.exp(-dist)
            hi, lo = halves(value)
            kmat_ref[q, i * own : (i + 1) * own, 0 : 2 * own] = hi
            kmat_ref[q, i * own : (i + 1) * own, 2 * own :] = lo
        return carry

    lax.fori_loop(0, n_plane // 2, build, 0)

    all_line(basis_ref, 10).wait_recv()
    for i in range(n_line):
        hi, lo = halves(basis_ref[i])
        wide_ref[:, i * own : (i + 1) * own] = hi
        wide_ref[:, (n_line + i) * own : (n_line + i + 1) * own] = lo

    def send_products(inbox, outbox, at, vectors, line):
        mine = stacked(vectors)
        for q in range(n_plane // 2):
            both = fold(dot_nn(mine, kmat_ref[q]))
            for half in range(2):
                t = 2 * q + 1 + half
                block = both[:, half * own : (half + 1) * own]
                slot, where = (inbox, in_plane) if t == n_plane else (outbox, t - 1)
                slot[where, 0:cols, :] = block
                if line is not None:
                    slot[where, cols : cols + 1, :] = line
                if t < n_plane:
                    remote(outbox.at[where], inbox.at[in_plane], at, plane_peers[t - 1]).start()

    def products(inbox, at):
        all_plane(inbox, at).wait_recv()
        return total(inbox, 0, n_plane)

    all_line(extra_ref.at[0], 6).wait_recv()
    leaf_lanes = of_line(0, 0)
    parts, stat = by_subtree(0)
    lanes = leaf_lanes + expand(own_coef(parts))
    send_products(prod_ref, out_ref, 11, lanes, None)
    direction = pick(lanes)
    rz_now = to_col(stat) + level_product(parts)

    image = products(prod_ref, 11) + noise_level * direction
    put(1, image, dots(direction, image))
    send_line(line_ref.at[1], 1)
    leaf_image = leaf(image)
    send_extra(1, leaf_image, image)
    cross(1)
    all_line(extra_ref.at[1], 7).wait_recv()
    leaf_step = of_line(1, 0)
    sums, stat = by_subtree(1)
    alpha_0 = rz_now / to_col(stat)
    parts = [a - alpha_0 * s for a, s in zip(parts, sums)]
    leaf_lanes = leaf_lanes - alpha_0 * leaf_step
    residual_lanes = of_line(0, 1) - alpha_0 * of_line(1, 1)
    leaf_line = to_row(dots(residual_lanes, leaf_lanes))
    lanes = leaf_lanes + expand(own_coef(parts))
    send_products(prod_stat_ref, out_stat_ref, 12, lanes, leaf_line)
    answer = alpha_0 * direction
    residual = rhs - alpha_0 * image
    leaf_res = leaf_res - alpha_0 * leaf_image
    precond = pick(lanes)
    levels = level_product(parts)

    product = products(prod_stat_ref, 12)
    leaf_total = to_col(product[cols:])
    rz_next = leaf_total + levels
    beta_0 = rz_next / rz_now
    rz_now = rz_next
    direction = precond + beta_0 * direction
    image = product[0:cols] + noise_level * precond + beta_0 * image
    leaf_image = leaf(image)
    put(2, image, dots(direction, image), dots(image, leaf_res), dots(image, leaf_image))
    send_line(line_ref.at[2], 2)
    cross(2)
    sums, stat = by_subtree(2)
    alpha_1 = rz_now / to_col(stat)
    sol_ref[...] = answer + alpha_1 * direction
    res_ref[...] = residual - alpha_1 * image
    leaf_last = leaf_total - alpha_1 * (2.0 * to_col(stat, 1) - alpha_1 * to_col(stat, 2))
    parts = [a - alpha_1 * s for a, s in zip(parts, sums)]
    beta_1 = (leaf_last + level_product(parts)) / rz_now
    for i, (alpha, beta) in enumerate(((alpha_0, beta_0), (alpha_1, beta_1))):
        coef_ref[0, i : i + 1, :] = to_row(alpha)[:, 0:cols]
        coef_ref[1, i : i + 1, :] = to_row(beta)[:, 0:cols]
    for at in range(3):
        all_line(line_ref.at[at], at).wait_send()
        all_plane(plane_ref.at[at], 3 + at).wait_send()
    for at in range(2):
        all_line(extra_ref.at[at], 6 + at).wait_send()
    all_line(pts_line_ref, 8).wait_send()
    all_plane(pts_plane_ref, 9).wait_send()
    all_line(basis_ref, 10).wait_send()
    all_plane(prod_ref, 11).wait_send()
    all_plane(prod_stat_ref, 12).wait_send()


def on_device(n_row, n_col, points, inverse_length, target, probe_bits, leaf_inverse, top_basis, sub_basis):
    low = math.gcd(n_col, 4)
    n_line, n_plane = low, n_row * (n_col // low)
    dim, own = points.shape
    cols = probe_bits.shape[0] + 1
    rank = top_basis.shape[0]
    vmem = pl.BlockSpec(memory_space=pltpu.VMEM)
    hbm = pl.BlockSpec(memory_space=pltpu.HBM)
    return pl.pallas_call(
        functools.partial(kernel, n_row, n_col, low, rank),
        out_shape=(
            jax.ShapeDtypeStruct((cols, own), F32),
            jax.ShapeDtypeStruct((cols, own), F32),
            jax.ShapeDtypeStruct((2, ITERS, cols), F32),
        ),
        in_specs=[hbm] * 7,
        out_specs=(vmem, vmem, vmem),
        scratch_shapes=[
            pltpu.VMEM(points.shape, F32),
            pltpu.VMEM((1, dim), F32),
            pltpu.VMEM(probe_bits.shape, jnp.int32),
            pltpu.VMEM(leaf_inverse.shape, F32),
            pltpu.VMEM((n_line, 2 * rank, own), F32),
            pltpu.VMEM((2 * rank, 2 * n_line * own), BF16),
            pltpu.VMEM((1, own), F32),
            pltpu.VMEM((cols, own), F32),
            pltpu.VMEM((n_line, dim, own), F32),
            pltpu.VMEM((n_plane, dim, own), F32),
            pltpu.VMEM((3, n_line, cols + 1, own), F32),
            pltpu.VMEM((2, n_line, 2 * cols, own), F32),
            pltpu.VMEM((3, n_plane, cols + 1, own), F32),
            pltpu.VMEM((n_plane, cols, own), F32),
            pltpu.VMEM((n_plane, cols + 1, own), F32),
            pltpu.VMEM((n_plane - 1, cols, own), F32),
            pltpu.VMEM((n_plane - 1, cols + 1, own), F32),
            pltpu.VMEM((n_plane // 2, n_line * own, 4 * own), BF16),
            pltpu.SemaphoreType.DMA((7,)),
            pltpu.SemaphoreType.DMA((13,)),
            pltpu.SemaphoreType.DMA((13,)),
        ],
        compiler_params=pltpu.CompilerParams(
            collective_id=0, has_side_effects=True, vmem_limit_bytes=62 * 1024 * 1024
        ),
    )(
        points,
        inverse_length.reshape(1, dim),
        target.reshape(1, own),
        probe_bits,
        leaf_inverse,
        top_basis,
        sub_basis,
    )


def solution(mesh):
    return jax.shard_map(
        functools.partial(on_device, mesh.shape["row"], mesh.shape["col"]),
        mesh=mesh,
        in_specs=(
            P(None, ("row", "col")),
            P(),
            P(("row", "col")),
            P(None, ("row", "col")),
            P(("row", "col"), None),
            P(None, ("row", "col")),
            P(None, ("row", "col")),
        ),
        out_specs=(P(None, ("row", "col")), P(None, ("row", "col")), P()),
        check_vma=False,
    )
```

```python
import functools
import math

import jax
import jax.numpy as jnp
from jax import lax
from jax.experimental import pallas as pl
from jax.experimental.pallas import tpu as pltpu
from jax.sharding import PartitionSpec as P

ITERS = 2
MESH = pl.DeviceIdType.MESH
F32 = jnp.float32
BF16 = jnp.bfloat16

noise_level = 0.5


def halves(x):
    hi = x.astype(BF16)
    return hi, (x - hi.astype(F32)).astype(BF16)


def thirds(x):
    hi = x.astype(BF16)
    rest = x - hi.astype(F32)
    mid = rest.astype(BF16)
    return hi, mid, (rest - mid.astype(F32)).astype(BF16)


def dot_nn(a, b):
    return lax.dot_general(a, b, (((1,), (0,)), ((), ())), preferred_element_type=F32)


def fold(out):
    rows, width = out.shape[0] // 2, out.shape[1] // 2
    return (
        (out[rows:, width:] + out[:rows, width:]) + out[rows:, :width]
    ) + out[:rows, :width]


def stacked(x):
    return jnp.concatenate(halves(x), axis=0)


def beside(x):
    return jnp.concatenate(halves(x), axis=1)


def kernel(
    n_row,
    n_col,
    low,
    rank,
    points_hbm,
    length_hbm,
    target_hbm,
    bits_hbm,
    leaf_hbm,
    top_hbm,
    sub_hbm,
    sol_ref,
    res_ref,
    coef_ref,
    points_ref,
    length_ref,
    bits_ref,
    leaf_ref,
    basis_ref,
    wide_ref,
    target_ref,
    rhs_ref,
    pts_line_ref,
    pts_plane_ref,
    line_ref,
    extra_ref,
    plane_ref,
    prod_ref,
    prod_stat_ref,
    out_ref,
    out_stat_ref,
    kmat_ref,
    load_sem,
    send_sem,
    recv_sem,
):
    n_high = n_col // low
    n_line, n_plane = low, n_row * n_high
    row, col = lax.axis_index("row"), lax.axis_index("col")
    high = lax.div(col, low)
    in_line = lax.rem(col, low)
    in_plane = row * n_high + high
    cols, own = rhs_ref.shape
    dim = points_ref.shape[0]

    line_peers = [(row, high * low + lax.rem(in_line + t, n_line)) for t in range(1, n_line)]
    plane_slots = [lax.rem(in_plane + t, n_plane) for t in range(n_plane)]
    plane_peers = [
        (lax.div(slot, n_high), lax.rem(slot, n_high) * low + in_line) for slot in plane_slots[1:]
    ]

    loads = [
        pltpu.make_async_copy(src, dst, load_sem.at[at])
        for at, (src, dst) in enumerate(
            (
                (points_hbm, points_ref),
                (length_hbm, length_ref),
                (target_hbm, target_ref),
                (bits_hbm, bits_ref),
                (top_hbm, basis_ref.at[in_line, pl.ds(0, rank)]),
                (sub_hbm, basis_ref.at[in_line, pl.ds(rank, rank)]),
                (leaf_hbm, leaf_ref),
            )
        )
    ]
    for load in loads:
        load.start()

    barrier = pltpu.get_barrier_semaphore()
    for peer in line_peers + plane_peers:
        pl.semaphore_signal(barrier, inc=1, device_id=peer, device_id_type=MESH)

    def remote(src, dst, at, device):
        return pltpu.make_async_remote_copy(
            src_ref=src,
            dst_ref=dst,
            send_sem=send_sem.at[at],
            recv_sem=recv_sem.at[at],
            device_id=device,
            device_id_type=MESH,
        )

    def send_line(buf, at):
        mine = buf.at[in_line]
        for peer in line_peers:
            remote(mine, mine, at, peer).start()

    def send_plane(buf, at):
        mine = buf.at[in_plane]
        for peer in plane_peers:
            remote(mine, mine, at, peer).start()

    def all_line(buf, at):
        some = buf.at[pl.ds(0, n_line - 1)]
        return remote(some, some, at, line_peers[0])

    def all_plane(buf, at):
        some = buf.at[pl.ds(0, n_plane - 1)]
        return remote(some, some, at, plane_peers[0])

    offset = lax.broadcasted_iota(jnp.int32, (cols, own), 1) - lax.broadcasted_iota(
        jnp.int32, (cols, own), 0
    )
    is_top = lax.broadcasted_iota(jnp.int32, (cols, 2 * rank), 1) < rank

    def to_row(*columns):
        spread = jnp.zeros((cols, own), F32)
        for at, column in enumerate(columns):
            spread = jnp.where(offset == at * cols, column, spread)
        return jnp.sum(spread, axis=0, keepdims=True)

    def to_col(line, at=0):
        return jnp.sum(jnp.where(offset == at * cols, line, 0.0), axis=1, keepdims=True)

    def dots(a, b):
        return jnp.sum(a * b, axis=1, keepdims=True)

    for load in loads[:4]:
        load.wait()
    rhs_ref[0:1, :] = target_ref[...]
    rhs_ref[1:cols, :] = 2.0 * bits_ref[...].astype(F32) - 1.0
    rhs = rhs_ref[...]
    inverse = jnp.sum(
        jnp.where(
            lax.broadcasted_iota(jnp.int32, (dim, dim), 0)
            == lax.broadcasted_iota(jnp.int32, (dim, dim), 1),
            length_ref[...],
            0.0,
        ),
        axis=1,
        keepdims=True,
    )
    scaled = points_ref[...] * inverse
    pts_line_ref[in_line] = scaled
    pts_plane_ref[in_plane] = scaled
    for load in loads[4:]:
        load.wait()
    basis_wide = beside(basis_ref[in_line].T)
    leaf_wide = beside(leaf_ref[...])

    def project(v):
        return fold(dot_nn(stacked(v), basis_wide))

    def expand(c):
        return fold(dot_nn(stacked(c), wide_ref[...]))

    def leaf(v):
        return fold(dot_nn(stacked(v), leaf_wide))

    def total(buf, first, count):
        out = buf[first]
        for i in range(first + 1, first + count):
            out = out + buf[i]
        return out

    def put(at, vector, *columns):
        line_ref[at, in_line, 0:cols, :] = project(vector)
        line_ref[at, in_line, cols : cols + 1, :] = to_row(*columns)

    def send_extra(at, *more):
        for i, part in enumerate(more):
            extra_ref[at, in_line, i * cols : (i + 1) * cols, :] = part
        send_line(extra_ref.at[at], 6 + at)

    def cross(at):
        all_line(line_ref.at[at], at).wait_recv()
        plane_ref[at, in_plane] = total(line_ref.at[at], 0, n_line)
        send_plane(plane_ref.at[at], 3 + at)

    def by_subtree(at):
        all_plane(plane_ref.at[at], 3 + at).wait_recv()
        sums = [total(plane_ref.at[at], i * n_high, n_high) for i in range(n_row)]
        return [s[0:cols] for s in sums], sum([s[cols:] for s in sums[1:]], sums[0][cols:])

    def of_line(at, which):
        rows = slice(which * cols, (which + 1) * cols)
        return jnp.concatenate([extra_ref[at, i, rows, :] for i in range(n_line)], axis=1)

    def pick(lanes):
        mine = lanes[:, 0:own]
        for i in range(1, n_line):
            mine = jnp.where(in_line == i, lanes[:, i * own : (i + 1) * own], mine)
        return mine

    def own_coef(parts):
        mine = parts[0]
        for i in range(1, n_row):
            mine = jnp.where(row == i, parts[i], mine)
        return jnp.where(is_top, sum(parts[1:], parts[0]), mine)

    def level_product(parts):
        every = sum(parts[1:], parts[0])
        squares = jnp.where(is_top, every * every, 0.0)
        for part in parts:
            squares = squares + jnp.where(is_top, 0.0, part * part)
        return jnp.sum(squares, axis=1, keepdims=True)

    leaf_res = leaf(rhs)
    put(0, rhs, dots(rhs, leaf_res))
    pl.semaphore_wait(barrier, n_line + n_plane - 2)
    send_line(line_ref.at[0], 0)
    send_line(pts_line_ref, 8)
    send_plane(pts_plane_ref, 9)
    send_extra(0, leaf_res, rhs)
    send_line(basis_ref, 10)

    def norm_rows(sq, first):
        pieces = [p.astype(F32) for p in thirds(sq)]
        line = lax.broadcasted_iota(jnp.int32, (16, sq.shape[1]), 0)
        out = jnp.where((line >= 3 - 3 * first) & (line < 6 - 3 * first), 1.0, 0.0)
        for at, piece in enumerate(pieces):
            out = jnp.where(line == 3 * first + at, piece, out)
        return out.astype(BF16)

    def features(x, order, first):
        pieces = thirds(x)
        sq = jnp.sum(x * x, axis=0, keepdims=True)
        return [pieces[at] for at in order], norm_rows(sq, first)

    all_line(pts_line_ref, 8).wait_recv()
    sources = jnp.concatenate([pts_line_ref[i] for i in range(n_line)], axis=1)
    src_parts, src_norm = features(sources, (0, 0, 0, 1, 1, 2), 0)
    src_feat = jnp.concatenate(
        [-2.0 * p.astype(F32) for p in src_parts] + [src_norm.astype(F32)], axis=0
    ).T.astype(BF16)
    cross(0)
    all_plane(pts_plane_ref, 9).wait_recv()

    def build(q, carry):
        pair = jnp.concatenate(
            [pts_plane_ref[lax.rem(in_plane + 2 * q + i, n_plane)] for i in (1, 2)], axis=1
        )
        far_parts, far_norm = features(pair, (0, 1, 2, 0, 1, 0), 1)
        far_feat = jnp.concatenate(far_parts + [far_norm], axis=0)
        for i in range(n_line):
            some = src_feat[i * own : (i + 1) * own]
            five_sq = jnp.maximum(5.0 * dot_nn(some, far_feat), 1e-30)
            dist = five_sq * lax.rsqrt(five_sq)
            value = (1.0 + dist + five_sq * (1.0 / 3.0)) * jnp.exp2(dist * (-1.0 / math.log(2.0)))
            hi, lo = halves(value)
            kmat_ref[q, i * own : (i + 1) * own, 0 : 2 * own] = hi
            kmat_ref[q, i * own : (i + 1) * own, 2 * own :] = lo
        return carry

    lax.fori_loop(0, n_plane // 2, build, 0)

    all_line(basis_ref, 10).wait_recv()
    for i in range(n_line):
        hi, lo = halves(basis_ref[i])
        wide_ref[:, i * own : (i + 1) * own] = hi
        wide_ref[:, (n_line + i) * own : (n_line + i + 1) * own] = lo

    def send_products(inbox, outbox, at, vectors, line):
        mine = stacked(vectors)
        for q in range(n_plane // 2):
            both = fold(dot_nn(mine, kmat_ref[q]))
            for half in range(2):
                t = 2 * q + 1 + half
                block = both[:, half * own : (half + 1) * own]
                slot, where = (inbox, in_plane) if t == n_plane else (outbox, t - 1)
                slot[where, 0:cols, :] = block
                if line is not None:
                    slot[where, cols : cols + 1, :] = line
                if t < n_plane:
                    remote(outbox.at[where], inbox.at[in_plane], at, plane_peers[t - 1]).start()

    def products(inbox, at):
        all_plane(inbox, at).wait_recv()
        return total(inbox, 0, n_plane)

    all_line(extra_ref.at[0], 6).wait_recv()
    leaf_lanes = of_line(0, 0)
    parts, stat = by_subtree(0)
    lanes = leaf_lanes + expand(own_coef(parts))
    send_products(prod_ref, out_ref, 11, lanes, None)
    direction = pick(lanes)
    rz_now = to_col(stat) + level_product(parts)

    image = products(prod_ref, 11) + noise_level * direction
    put(1, image, dots(direction, image))
    send_line(line_ref.at[1], 1)
    leaf_image = leaf(image)
    send_extra(1, leaf_image, image)
    cross(1)
    all_line(extra_ref.at[1], 7).wait_recv()
    leaf_step = of_line(1, 0)
    sums, stat = by_subtree(1)
    alpha_0 = rz_now / to_col(stat)
    parts = [a - alpha_0 * s for a, s in zip(parts, sums)]
    leaf_lanes = leaf_lanes - alpha_0 * leaf_step
    residual_lanes = of_line(0, 1) - alpha_0 * of_line(1, 1)
    leaf_line = to_row(dots(residual_lanes, leaf_lanes))
    lanes = leaf_lanes + expand(own_coef(parts))
    send_products(prod_stat_ref, out_stat_ref, 12, lanes, leaf_line)
    answer = alpha_0 * direction
    residual = rhs - alpha_0 * image
    leaf_res = leaf_res - alpha_0 * leaf_image
    precond = pick(lanes)
    levels = level_product(parts)

    product = products(prod_stat_ref, 12)
    leaf_total = to_col(product[cols:])
    rz_next = leaf_total + levels
    beta_0 = rz_next / rz_now
    rz_now = rz_next
    direction = precond + beta_0 * direction
    image = product[0:cols] + noise_level * precond + beta_0 * image
    leaf_image = leaf(image)
    put(2, image, dots(direction, image), dots(image, leaf_res), dots(image, leaf_image))
    send_line(line_ref.at[2], 2)
    cross(2)
    sums, stat = by_subtree(2)
    alpha_1 = rz_now / to_col(stat)
    sol_ref[...] = answer + alpha_1 * direction
    res_ref[...] = residual - alpha_1 * image
    leaf_last = leaf_total - alpha_1 * (2.0 * to_col(stat, 1) - alpha_1 * to_col(stat, 2))
    parts = [a - alpha_1 * s for a, s in zip(parts, sums)]
    beta_1 = (leaf_last + level_product(parts)) / rz_now
    for i, (alpha, beta) in enumerate(((alpha_0, beta_0), (alpha_1, beta_1))):
        coef_ref[0, i : i + 1, :] = to_row(alpha)[:, 0:cols]
        coef_ref[1, i : i + 1, :] = to_row(beta)[:, 0:cols]
    for at in range(3):
        all_line(line_ref.at[at], at).wait_send()
        all_plane(plane_ref.at[at], 3 + at).wait_send()
    for at in range(2):
        all_line(extra_ref.at[at], 6 + at).wait_send()
    all_line(pts_line_ref, 8).wait_send()
    all_plane(pts_plane_ref, 9).wait_send()
    all_line(basis_ref, 10).wait_send()
    all_plane(prod_ref, 11).wait_send()
    all_plane(prod_stat_ref, 12).wait_send()


def on_device(n_row, n_col, points, inverse_length, target, probe_bits, leaf_inverse, top_basis, sub_basis):
    low = math.gcd(n_col, 4)
    n_line, n_plane = low, n_row * (n_col // low)
    dim, own = points.shape
    cols = probe_bits.shape[0] + 1
    rank = top_basis.shape[0]
    vmem = pl.BlockSpec(memory_space=pltpu.VMEM)
    hbm = pl.BlockSpec(memory_space=pltpu.HBM)
    return pl.pallas_call(
        functools.partial(kernel, n_row, n_col, low, rank),
        out_shape=(
            jax.ShapeDtypeStruct((cols, own), F32),
            jax.ShapeDtypeStruct((cols, own), F32),
            jax.ShapeDtypeStruct((2, ITERS, cols), F32),
        ),
        in_specs=[hbm] * 7,
        out_specs=(vmem, vmem, vmem),
        scratch_shapes=[
            pltpu.VMEM(points.shape, F32),
            pltpu.VMEM((1, dim), F32),
            pltpu.VMEM(probe_bits.shape, jnp.int32),
            pltpu.VMEM(leaf_inverse.shape, F32),
            pltpu.VMEM((n_line, 2 * rank, own), F32),
            pltpu.VMEM((2 * rank, 2 * n_line * own), BF16),
            pltpu.VMEM((1, own), F32),
            pltpu.VMEM((cols, own), F32),
            pltpu.VMEM((n_line, dim, own), F32),
            pltpu.VMEM((n_plane, dim, own), F32),
            pltpu.VMEM((3, n_line, cols + 1, own), F32),
            pltpu.VMEM((2, n_line, 2 * cols, own), F32),
            pltpu.VMEM((3, n_plane, cols + 1, own), F32),
            pltpu.VMEM((n_plane, cols, own), F32),
            pltpu.VMEM((n_plane, cols + 1, own), F32),
            pltpu.VMEM((n_plane - 1, cols, own), F32),
            pltpu.VMEM((n_plane - 1, cols + 1, own), F32),
            pltpu.VMEM((n_plane // 2, n_line * own, 4 * own), BF16),
            pltpu.SemaphoreType.DMA((7,)),
            pltpu.SemaphoreType.DMA((13,)),
            pltpu.SemaphoreType.DMA((13,)),
        ],
        compiler_params=pltpu.CompilerParams(
            collective_id=0, has_side_effects=True, vmem_limit_bytes=55202 * 1024
        ),
    )(
        points,
        inverse_length.reshape(1, dim),
        target.reshape(1, own),
        probe_bits,
        leaf_inverse,
        top_basis,
        sub_basis,
    )


def solution(mesh):
    return jax.shard_map(
        functools.partial(on_device, mesh.shape["row"], mesh.shape["col"]),
        mesh=mesh,
        in_specs=(
            P(None, ("row", "col")),
            P(),
            P(("row", "col")),
            P(None, ("row", "col")),
            P(("row", "col"), None),
            P(None, ("row", "col")),
            P(None, ("row", "col")),
        ),
        out_specs=(P(None, ("row", "col")), P(None, ("row", "col")), P()),
        check_vma=False,
    )
```

```python
import functools
import math

import jax
import jax.numpy as jnp
from jax import lax
from jax.experimental import pallas as pl
from jax.experimental.pallas import tpu as pltpu
from jax.sharding import PartitionSpec as P

ITERS = 2
MESH = pl.DeviceIdType.MESH
F32 = jnp.float32
BF16 = jnp.bfloat16

noise_level = 0.5


def halves(x):
    hi = x.astype(BF16)
    return hi, (x - hi.astype(F32)).astype(BF16)


def thirds(x):
    hi = x.astype(BF16)
    rest = x - hi.astype(F32)
    mid = rest.astype(BF16)
    return hi, mid, (rest - mid.astype(F32)).astype(BF16)


def dot_nn(a, b):
    return lax.dot_general(a, b, (((1,), (0,)), ((), ())), preferred_element_type=F32)


def fold(out):
    rows, width = out.shape[0] // 2, out.shape[1] // 2
    return (
        (out[rows:, width:] + out[:rows, width:]) + out[rows:, :width]
    ) + out[:rows, :width]


def stacked(x):
    return jnp.concatenate(halves(x), axis=0)


def beside(x):
    return jnp.concatenate(halves(x), axis=1)


def kernel(
    n_row,
    n_col,
    low,
    rank,
    points_hbm,
    length_hbm,
    target_hbm,
    bits_hbm,
    leaf_hbm,
    top_hbm,
    sub_hbm,
    sol_ref,
    res_ref,
    coef_ref,
    points_ref,
    length_ref,
    bits_ref,
    leaf_ref,
    basis_ref,
    wide_ref,
    target_ref,
    rhs_ref,
    pts_line_ref,
    pts_plane_ref,
    line_ref,
    extra_ref,
    plane_ref,
    prod_ref,
    prod_stat_ref,
    out_ref,
    out_stat_ref,
    kmat_ref,
    load_sem,
    send_sem,
    recv_sem,
    pts_sem,
):
    n_high = n_col // low
    n_line, n_plane = low, n_row * n_high
    row, col = lax.axis_index("row"), lax.axis_index("col")
    high = lax.div(col, low)
    in_line = lax.rem(col, low)
    in_plane = row * n_high + high
    cols, own = rhs_ref.shape
    dim = points_ref.shape[0]

    line_peers = [(row, high * low + lax.rem(in_line + t, n_line)) for t in range(1, n_line)]
    plane_slots = [lax.rem(in_plane + t, n_plane) for t in range(n_plane)]
    plane_peers = [
        (lax.div(slot, n_high), lax.rem(slot, n_high) * low + in_line) for slot in plane_slots[1:]
    ]

    barrier = pltpu.get_barrier_semaphore()
    for peer in line_peers + plane_peers:
        pl.semaphore_signal(barrier, inc=1, device_id=peer, device_id_type=MESH)

    loads = [
        pltpu.make_async_copy(src, dst, load_sem.at[at])
        for at, (src, dst) in enumerate(
            (
                (points_hbm, points_ref),
                (length_hbm, length_ref),
                (target_hbm, target_ref),
                (bits_hbm, bits_ref),
                (top_hbm, basis_ref.at[in_line, pl.ds(0, rank)]),
                (sub_hbm, basis_ref.at[in_line, pl.ds(rank, rank)]),
                (leaf_hbm, leaf_ref),
            )
        )
    ]
    for load in loads:
        load.start()

    def remote(src, dst, at, device):
        return pltpu.make_async_remote_copy(
            src_ref=src,
            dst_ref=dst,
            send_sem=send_sem.at[at],
            recv_sem=recv_sem.at[at],
            device_id=device,
            device_id_type=MESH,
        )

    def send_line(buf, at):
        mine = buf.at[in_line]
        for peer in line_peers:
            remote(mine, mine, at, peer).start()

    def send_plane(buf, at):
        mine = buf.at[in_plane]
        for peer in plane_peers:
            remote(mine, mine, at, peer).start()

    def all_line(buf, at):
        some = buf.at[pl.ds(0, n_line - 1)]
        return remote(some, some, at, line_peers[0])

    def all_plane(buf, at):
        some = buf.at[pl.ds(0, n_plane - 1)]
        return remote(some, some, at, plane_peers[0])

    offset = lax.broadcasted_iota(jnp.int32, (cols, own), 1) - lax.broadcasted_iota(
        jnp.int32, (cols, own), 0
    )
    is_top = lax.broadcasted_iota(jnp.int32, (cols, 2 * rank), 1) < rank

    def to_row(*columns):
        spread = jnp.zeros((cols, own), F32)
        for at, column in enumerate(columns):
            spread = jnp.where(offset == at * cols, column, spread)
        return jnp.sum(spread, axis=0, keepdims=True)

    def to_col(line, at=0):
        return jnp.sum(jnp.where(offset == at * cols, line, 0.0), axis=1, keepdims=True)

    def dots(a, b):
        return jnp.sum(a * b, axis=1, keepdims=True)

    for load in loads[:4]:
        load.wait()
    rhs_ref[0:1, :] = target_ref[...]
    rhs_ref[1:cols, :] = 2.0 * bits_ref[...].astype(F32) - 1.0
    rhs = rhs_ref[...]
    inverse = jnp.sum(
        jnp.where(
            lax.broadcasted_iota(jnp.int32, (dim, dim), 0)
            == lax.broadcasted_iota(jnp.int32, (dim, dim), 1),
            length_ref[...],
            0.0,
        ),
        axis=1,
        keepdims=True,
    )
    scaled = points_ref[...] * inverse
    pts_line_ref[in_line] = scaled
    pts_plane_ref[in_plane] = scaled
    for load in loads[4:]:
        load.wait()
    basis_wide = beside(basis_ref[in_line].T)
    leaf_wide = beside(leaf_ref[...])

    def project(v):
        return fold(dot_nn(stacked(v), basis_wide))

    def expand(c):
        return fold(dot_nn(stacked(c), wide_ref[...]))

    def leaf(v):
        return fold(dot_nn(stacked(v), leaf_wide))

    def total(buf, first, count):
        out = buf[first]
        for i in range(first + 1, first + count):
            out = out + buf[i]
        return out

    def put(at, vector, *columns):
        line_ref[at, in_line, 0:cols, :] = project(vector)
        line_ref[at, in_line, cols : cols + 1, :] = to_row(*columns)

    def send_extra(at, *more):
        for i, part in enumerate(more):
            extra_ref[at, in_line, i * cols : (i + 1) * cols, :] = part
        send_line(extra_ref.at[at], 6 + at)

    def cross(at):
        all_line(line_ref.at[at], at).wait_recv()
        plane_ref[at, in_plane] = total(line_ref.at[at], 0, n_line)
        send_plane(plane_ref.at[at], 3 + at)

    def by_subtree(at):
        all_plane(plane_ref.at[at], 3 + at).wait_recv()
        sums = [total(plane_ref.at[at], i * n_high, n_high) for i in range(n_row)]
        return [s[0:cols] for s in sums], sum([s[cols:] for s in sums[1:]], sums[0][cols:])

    def of_line(at, which):
        rows = slice(which * cols, (which + 1) * cols)
        return jnp.concatenate([extra_ref[at, i, rows, :] for i in range(n_line)], axis=1)

    def pick(lanes):
        mine = lanes[:, 0:own]
        for i in range(1, n_line):
            mine = jnp.where(in_line == i, lanes[:, i * own : (i + 1) * own], mine)
        return mine

    def own_coef(parts):
        mine = parts[0]
        for i in range(1, n_row):
            mine = jnp.where(row == i, parts[i], mine)
        return jnp.where(is_top, sum(parts[1:], parts[0]), mine)

    def level_product(parts):
        every = sum(parts[1:], parts[0])
        squares = jnp.where(is_top, every * every, 0.0)
        for part in parts:
            squares = squares + jnp.where(is_top, 0.0, part * part)
        return jnp.sum(squares, axis=1, keepdims=True)

    def points_to(t, peer):
        return pltpu.make_async_remote_copy(
            src_ref=pts_plane_ref.at[in_plane],
            dst_ref=pts_plane_ref.at[in_plane],
            send_sem=send_sem.at[9],
            recv_sem=pts_sem.at[t],
            device_id=peer,
            device_id_type=MESH,
        )

    leaf_res = leaf(rhs)
    put(0, rhs, dots(rhs, leaf_res))
    pl.semaphore_wait(barrier, n_line + n_plane - 2)
    send_line(line_ref.at[0], 0)
    send_line(pts_line_ref, 8)
    for t, peer in enumerate(plane_peers, 1):
        points_to(t, peer).start()
    send_extra(0, leaf_res, rhs)
    send_line(basis_ref, 10)
    cross(0)

    def norm_rows(sq, first):
        pieces = [p.astype(F32) for p in thirds(sq)]
        line = lax.broadcasted_iota(jnp.int32, (16, sq.shape[1]), 0)
        out = jnp.where((line >= 3 - 3 * first) & (line < 6 - 3 * first), 1.0, 0.0)
        for at, piece in enumerate(pieces):
            out = jnp.where(line == 3 * first + at, piece, out)
        return out.astype(BF16)

    def features(x, order, first):
        pieces = thirds(x)
        sq = jnp.sum(x * x, axis=0, keepdims=True)
        return [pieces[at] for at in order], norm_rows(sq, first)

    all_line(pts_line_ref, 8).wait_recv()
    sources = jnp.concatenate([pts_line_ref[i] for i in range(n_line)], axis=1)
    src_parts, src_norm = features(sources, (0, 0, 0, 1, 1, 2), 0)
    src_feat = jnp.concatenate(
        [-2.0 * p.astype(F32) for p in src_parts] + [src_norm.astype(F32)], axis=0
    ).T.astype(BF16)

    def build(q, carry, arriving=2):
        for i in range(arriving):
            points_to(n_plane - 1 - 2 * q - i, plane_peers[0]).wait_recv()
        pair = jnp.concatenate(
            [pts_plane_ref[lax.rem(in_plane + 2 * q + i, n_plane)] for i in (1, 2)], axis=1
        )
        far_parts, far_norm = features(pair, (0, 1, 2, 0, 1, 0), 1)
        far_feat = jnp.concatenate(far_parts + [far_norm], axis=0)
        for i in range(n_line):
            some = src_feat[i * own : (i + 1) * own]
            five_sq = jnp.maximum(5.0 * dot_nn(some, far_feat), 1e-30)
            dist = five_sq * lax.rsqrt(five_sq)
            value = (1.0 + dist + five_sq * (1.0 / 3.0)) * jnp.exp2(dist * (-1.0 / math.log(2.0)))
            hi, lo = halves(value)
            kmat_ref[q, i * own : (i + 1) * own, 0 : 2 * own] = hi
            kmat_ref[q, i * own : (i + 1) * own, 2 * own :] = lo
        return carry

    lax.fori_loop(0, n_plane // 2 - 1, build, 0)
    build(n_plane // 2 - 1, 0, 1)

    all_line(basis_ref, 10).wait_recv()
    for i in range(n_line):
        hi, lo = halves(basis_ref[i])
        wide_ref[:, i * own : (i + 1) * own] = hi
        wide_ref[:, (n_line + i) * own : (n_line + i + 1) * own] = lo

    def send_products(inbox, outbox, at, vectors, line):
        mine = stacked(vectors)
        for q in range(n_plane // 2):
            both = fold(dot_nn(mine, kmat_ref[q]))
            for half in range(2):
                t = 2 * q + 1 + half
                block = both[:, half * own : (half + 1) * own]
                slot, where = (inbox, in_plane) if t == n_plane else (outbox, t - 1)
                slot[where, 0:cols, :] = block
                if line is not None:
                    slot[where, cols : cols + 1, :] = line
                if t < n_plane:
                    remote(outbox.at[where], inbox.at[in_plane], at, plane_peers[t - 1]).start()

    def products(inbox, at):
        all_plane(inbox, at).wait_recv()
        return total(inbox, 0, n_plane)

    all_line(extra_ref.at[0], 6).wait_recv()
    leaf_lanes = of_line(0, 0)
    parts, stat = by_subtree(0)
    lanes = leaf_lanes + expand(own_coef(parts))
    send_products(prod_ref, out_ref, 11, lanes, None)
    direction = pick(lanes)
    rz_now = to_col(stat) + level_product(parts)

    image = products(prod_ref, 11) + noise_level * direction
    put(1, image, dots(direction, image))
    send_line(line_ref.at[1], 1)
    leaf_image = leaf(image)
    send_extra(1, leaf_image, image)
    cross(1)
    all_line(extra_ref.at[1], 7).wait_recv()
    leaf_step = of_line(1, 0)
    sums, stat = by_subtree(1)
    alpha_0 = rz_now / to_col(stat)
    parts = [a - alpha_0 * s for a, s in zip(parts, sums)]
    leaf_lanes = leaf_lanes - alpha_0 * leaf_step
    residual_lanes = of_line(0, 1) - alpha_0 * of_line(1, 1)
    leaf_line = to_row(dots(residual_lanes, leaf_lanes))
    lanes = leaf_lanes + expand(own_coef(parts))
    send_products(prod_stat_ref, out_stat_ref, 12, lanes, leaf_line)
    answer = alpha_0 * direction
    residual = rhs - alpha_0 * image
    leaf_res = leaf_res - alpha_0 * leaf_image
    precond = pick(lanes)
    levels = level_product(parts)

    product = products(prod_stat_ref, 12)
    leaf_total = to_col(product[cols:])
    rz_next = leaf_total + levels
    beta_0 = rz_next / rz_now
    rz_now = rz_next
    direction = precond + beta_0 * direction
    image = product[0:cols] + noise_level * precond + beta_0 * image
    leaf_image = leaf(image)
    put(2, image, dots(direction, image), dots(image, leaf_res), dots(image, leaf_image))
    send_line(line_ref.at[2], 2)
    cross(2)
    sums, stat = by_subtree(2)
    alpha_1 = rz_now / to_col(stat)
    sol_ref[...] = answer + alpha_1 * direction
    res_ref[...] = residual - alpha_1 * image
    leaf_last = leaf_total - alpha_1 * (2.0 * to_col(stat, 1) - alpha_1 * to_col(stat, 2))
    parts = [a - alpha_1 * s for a, s in zip(parts, sums)]
    beta_1 = (leaf_last + level_product(parts)) / rz_now
    for i, (alpha, beta) in enumerate(((alpha_0, beta_0), (alpha_1, beta_1))):
        coef_ref[0, i : i + 1, :] = to_row(alpha)[:, 0:cols]
        coef_ref[1, i : i + 1, :] = to_row(beta)[:, 0:cols]
    for at in range(3):
        all_line(line_ref.at[at], at).wait_send()
        all_plane(plane_ref.at[at], 3 + at).wait_send()
    for at in range(2):
        all_line(extra_ref.at[at], 6 + at).wait_send()
    all_line(pts_line_ref, 8).wait_send()
    all_plane(pts_plane_ref, 9).wait_send()
    all_line(basis_ref, 10).wait_send()
    all_plane(prod_ref, 11).wait_send()
    all_plane(prod_stat_ref, 12).wait_send()


def on_device(n_row, n_col, points, inverse_length, target, probe_bits, leaf_inverse, top_basis, sub_basis):
    low = math.gcd(n_col, 4)
    n_line, n_plane = low, n_row * (n_col // low)
    dim, own = points.shape
    cols = probe_bits.shape[0] + 1
    rank = top_basis.shape[0]
    vmem = pl.BlockSpec(memory_space=pltpu.VMEM)
    hbm = pl.BlockSpec(memory_space=pltpu.HBM)
    return pl.pallas_call(
        functools.partial(kernel, n_row, n_col, low, rank),
        out_shape=(
            jax.ShapeDtypeStruct((cols, own), F32),
            jax.ShapeDtypeStruct((cols, own), F32),
            jax.ShapeDtypeStruct((2, ITERS, cols), F32),
        ),
        in_specs=[hbm] * 7,
        out_specs=(vmem, vmem, vmem),
        scratch_shapes=[
            pltpu.VMEM(points.shape, F32),
            pltpu.VMEM((1, dim), F32),
            pltpu.VMEM(probe_bits.shape, jnp.int32),
            pltpu.VMEM(leaf_inverse.shape, F32),
            pltpu.VMEM((n_line, 2 * rank, own), F32),
            pltpu.VMEM((2 * rank, 2 * n_line * own), BF16),
            pltpu.VMEM((1, own), F32),
            pltpu.VMEM((cols, own), F32),
            pltpu.VMEM((n_line, dim, own), F32),
            pltpu.VMEM((n_plane, dim, own), F32),
            pltpu.VMEM((3, n_line, cols + 1, own), F32),
            pltpu.VMEM((2, n_line, 2 * cols, own), F32),
            pltpu.VMEM((3, n_plane, cols + 1, own), F32),
            pltpu.VMEM((n_plane, cols, own), F32),
            pltpu.VMEM((n_plane, cols + 1, own), F32),
            pltpu.VMEM((n_plane - 1, cols, own), F32),
            pltpu.VMEM((n_plane - 1, cols + 1, own), F32),
            pltpu.VMEM((n_plane // 2, n_line * own, 4 * own), BF16),
            pltpu.SemaphoreType.DMA((7,)),
            pltpu.SemaphoreType.DMA((13,)),
            pltpu.SemaphoreType.DMA((13,)),
            pltpu.SemaphoreType.DMA((n_plane,)),
        ],
        compiler_params=pltpu.CompilerParams(
            collective_id=0, has_side_effects=True, vmem_limit_bytes=55202 * 1024
        ),
    )(
        points,
        inverse_length.reshape(1, dim),
        target.reshape(1, own),
        probe_bits,
        leaf_inverse,
        top_basis,
        sub_basis,
    )


def solution(mesh):
    return jax.shard_map(
        functools.partial(on_device, mesh.shape["row"], mesh.shape["col"]),
        mesh=mesh,
        in_specs=(
            P(None, ("row", "col")),
            P(),
            P(("row", "col")),
            P(None, ("row", "col")),
            P(("row", "col"), None),
            P(None, ("row", "col")),
            P(None, ("row", "col")),
        ),
        out_specs=(P(None, ("row", "col")), P(None, ("row", "col")), P()),
        check_vma=False,
    )
```

```python
import functools
import math

import jax
import jax.numpy as jnp
from jax import lax
from jax.experimental import pallas as pl
from jax.experimental.pallas import tpu as pltpu
from jax.sharding import PartitionSpec as P

ITERS = 2
MESH = pl.DeviceIdType.MESH
F32 = jnp.float32
BF16 = jnp.bfloat16

noise_level = 0.5


def halves(x):
    hi = x.astype(BF16)
    return hi, (x - hi.astype(F32)).astype(BF16)


def thirds(x):
    hi = x.astype(BF16)
    rest = x - hi.astype(F32)
    mid = rest.astype(BF16)
    return hi, mid, (rest - mid.astype(F32)).astype(BF16)


def dot_nn(a, b):
    return lax.dot_general(a, b, (((1,), (0,)), ((), ())), preferred_element_type=F32)


def fold(out):
    rows, width = out.shape[0] // 2, out.shape[1] // 2
    return (
        (out[rows:, width:] + out[:rows, width:]) + out[rows:, :width]
    ) + out[:rows, :width]


def stacked(x):
    return jnp.concatenate(halves(x), axis=0)


def beside(x):
    return jnp.concatenate(halves(x), axis=1)


def kernel(
    n_row,
    n_col,
    low,
    rank,
    points_hbm,
    length_hbm,
    target_hbm,
    bits_hbm,
    leaf_hbm,
    top_hbm,
    sub_hbm,
    sol_ref,
    res_ref,
    coef_ref,
    points_ref,
    length_ref,
    bits_ref,
    leaf_ref,
    basis_ref,
    wide_ref,
    target_ref,
    rhs_ref,
    pts_line_ref,
    pts_plane_ref,
    line_ref,
    extra_ref,
    plane_ref,
    prod_ref,
    prod_stat_ref,
    out_ref,
    out_stat_ref,
    kmat_ref,
    load_sem,
    send_sem,
    recv_sem,
    pts_sem,
):
    n_high = n_col // low
    n_line, n_plane = low, n_row * n_high
    row, col = lax.axis_index("row"), lax.axis_index("col")
    high = lax.div(col, low)
    in_line = lax.rem(col, low)
    in_plane = row * n_high + high
    cols, own = rhs_ref.shape
    dim = points_ref.shape[0]

    line_peers = [(row, high * low + lax.rem(in_line + t, n_line)) for t in range(1, n_line)]
    plane_slots = [lax.rem(in_plane + t, n_plane) for t in range(n_plane)]
    plane_peers = [
        (lax.div(slot, n_high), lax.rem(slot, n_high) * low + in_line) for slot in plane_slots[1:]
    ]

    barrier = pltpu.get_barrier_semaphore()
    for peer in line_peers + plane_peers:
        pl.semaphore_signal(barrier, inc=1, device_id=peer, device_id_type=MESH)

    loads = [
        pltpu.make_async_copy(src, dst, load_sem.at[at])
        for at, (src, dst) in enumerate(
            (
                (points_hbm, points_ref),
                (length_hbm, length_ref),
                (target_hbm, target_ref),
                (bits_hbm, bits_ref),
                (top_hbm, basis_ref.at[in_line, pl.ds(0, rank)]),
                (sub_hbm, basis_ref.at[in_line, pl.ds(rank, rank)]),
                (leaf_hbm, leaf_ref),
            )
        )
    ]
    for load in loads:
        load.start()

    def remote(src, dst, at, device):
        return pltpu.make_async_remote_copy(
            src_ref=src,
            dst_ref=dst,
            send_sem=send_sem.at[at],
            recv_sem=recv_sem.at[at],
            device_id=device,
            device_id_type=MESH,
        )

    def send_line(buf, at):
        mine = buf.at[in_line]
        for peer in line_peers:
            remote(mine, mine, at, peer).start()

    def send_plane(buf, at):
        mine = buf.at[in_plane]
        for peer in plane_peers:
            remote(mine, mine, at, peer).start()

    def all_line(buf, at):
        some = buf.at[pl.ds(0, n_line - 1)]
        return remote(some, some, at, line_peers[0])

    def all_plane(buf, at):
        some = buf.at[pl.ds(0, n_plane - 1)]
        return remote(some, some, at, plane_peers[0])

    offset = lax.broadcasted_iota(jnp.int32, (cols, own), 1) - lax.broadcasted_iota(
        jnp.int32, (cols, own), 0
    )
    is_top = lax.broadcasted_iota(jnp.int32, (cols, 2 * rank), 1) < rank

    def to_row(*columns):
        spread = jnp.zeros((cols, own), F32)
        for at, column in enumerate(columns):
            spread = jnp.where(offset == at * cols, column, spread)
        return jnp.sum(spread, axis=0, keepdims=True)

    def to_col(line, at=0):
        return jnp.sum(jnp.where(offset == at * cols, line, 0.0), axis=1, keepdims=True)

    def dots(a, b):
        return jnp.sum(a * b, axis=1, keepdims=True)

    for load in loads[:4]:
        load.wait()
    rhs_ref[0:1, :] = target_ref[...]
    rhs_ref[1:cols, :] = 2.0 * bits_ref[...].astype(F32) - 1.0
    rhs = rhs_ref[...]
    inverse = jnp.sum(
        jnp.where(
            lax.broadcasted_iota(jnp.int32, (dim, dim), 0)
            == lax.broadcasted_iota(jnp.int32, (dim, dim), 1),
            length_ref[...],
            0.0,
        ),
        axis=1,
        keepdims=True,
    )
    scaled = points_ref[...] * inverse
    pts_line_ref[in_line] = scaled
    pts_plane_ref[in_plane] = scaled
    for load in loads[4:]:
        load.wait()
    basis_wide = beside(basis_ref[in_line].T)
    leaf_wide = beside(leaf_ref[...])

    def project(v):
        return fold(dot_nn(stacked(v), basis_wide))

    def expand(c):
        return fold(dot_nn(stacked(c), wide_ref[...]))

    def leaf(v):
        return fold(dot_nn(stacked(v), leaf_wide))

    def total(buf, first, count):
        out = buf[first]
        for i in range(first + 1, first + count):
            out = out + buf[i]
        return out

    def put(at, vector, *columns):
        line_ref[at, in_line, 0:cols, :] = project(vector)
        line_ref[at, in_line, cols : cols + 1, :] = to_row(*columns)

    def send_extra(at, *more):
        for i, part in enumerate(more):
            extra_ref[at, in_line, i * cols : (i + 1) * cols, :] = part
        send_line(extra_ref.at[at], 6 + at)

    def cross(at):
        all_line(line_ref.at[at], at).wait_recv()
        plane_ref[at, in_plane] = total(line_ref.at[at], 0, n_line)
        send_plane(plane_ref.at[at], 3 + at)

    def by_subtree(at):
        all_plane(plane_ref.at[at], 3 + at).wait_recv()
        sums = [total(plane_ref.at[at], i * n_high, n_high) for i in range(n_row)]
        return [s[0:cols] for s in sums], sum([s[cols:] for s in sums[1:]], sums[0][cols:])

    def of_line(at, which):
        rows = slice(which * cols, (which + 1) * cols)
        return jnp.concatenate([extra_ref[at, i, rows, :] for i in range(n_line)], axis=1)

    def pick(lanes):
        mine = lanes[:, 0:own]
        for i in range(1, n_line):
            mine = jnp.where(in_line == i, lanes[:, i * own : (i + 1) * own], mine)
        return mine

    def own_coef(parts):
        mine = parts[0]
        for i in range(1, n_row):
            mine = jnp.where(row == i, parts[i], mine)
        return jnp.where(is_top, sum(parts[1:], parts[0]), mine)

    def level_product(parts):
        every = sum(parts[1:], parts[0])
        squares = jnp.where(is_top, every * every, 0.0)
        for part in parts:
            squares = squares + jnp.where(is_top, 0.0, part * part)
        return jnp.sum(squares, axis=1, keepdims=True)

    def points_to(t, peer):
        return pltpu.make_async_remote_copy(
            src_ref=pts_plane_ref.at[in_plane],
            dst_ref=pts_plane_ref.at[in_plane],
            send_sem=send_sem.at[9],
            recv_sem=pts_sem.at[t],
            device_id=peer,
            device_id_type=MESH,
        )

    leaf_res = leaf(rhs)
    put(0, rhs, dots(rhs, leaf_res))
    pl.semaphore_wait(barrier, n_line + n_plane - 2)
    send_line(line_ref.at[0], 0)
    send_line(pts_line_ref, 8)
    for t, peer in enumerate(plane_peers, 1):
        points_to(t, peer).start()
    send_extra(0, leaf_res, rhs)
    send_line(basis_ref, 10)
    cross(0)

    def norm_rows(sq, first):
        pieces = [p.astype(F32) for p in thirds(sq)]
        line = lax.broadcasted_iota(jnp.int32, (16, sq.shape[1]), 0)
        out = jnp.where((line >= 3 - 3 * first) & (line < 6 - 3 * first), 1.0, 0.0)
        for at, piece in enumerate(pieces):
            out = jnp.where(line == 3 * first + at, piece, out)
        return out.astype(BF16)

    def features(x, order, first):
        pieces = thirds(x)
        sq = jnp.sum(x * x, axis=0, keepdims=True)
        return [pieces[at] for at in order], norm_rows(sq, first)

    all_line(pts_line_ref, 8).wait_recv()
    sources = jnp.concatenate([pts_line_ref[i] for i in range(n_line)], axis=1)
    src_parts, src_norm = features(sources, (0, 0, 0, 1, 1, 2), 0)
    src_feat = jnp.concatenate(
        [-2.0 * p.astype(F32) for p in src_parts] + [src_norm.astype(F32)], axis=0
    ).T.astype(BF16)

    def build(q, carry, arriving=2):
        for i in range(arriving):
            points_to(n_plane - 1 - 2 * q - i, plane_peers[0]).wait_recv()
        pair = jnp.concatenate(
            [pts_plane_ref[lax.rem(in_plane + 2 * q + i, n_plane)] for i in (1, 2)], axis=1
        )
        far_parts, far_norm = features(pair, (0, 1, 2, 0, 1, 0), 1)
        far_feat = jnp.concatenate(far_parts + [far_norm], axis=0)
        for i in range(n_line):
            some = src_feat[i * own : (i + 1) * own]
            five_sq = jnp.maximum(5.0 * dot_nn(some, far_feat), 1e-30)
            dist = five_sq * lax.rsqrt(five_sq)
            value = (1.0 + dist + five_sq * (1.0 / 3.0)) * jnp.exp2(dist * (-1.0 / math.log(2.0)))
            hi, lo = halves(value)
            kmat_ref[q, i * own : (i + 1) * own, 0 : 2 * own] = hi
            kmat_ref[q, i * own : (i + 1) * own, 2 * own :] = lo
        return carry

    lax.fori_loop(0, n_plane // 2 - 1, build, 0)
    build(n_plane // 2 - 1, 0, 1)

    all_line(basis_ref, 10).wait_recv()
    for i in range(n_line):
        hi, lo = halves(basis_ref[i])
        wide_ref[:, i * own : (i + 1) * own] = hi
        wide_ref[:, (n_line + i) * own : (n_line + i + 1) * own] = lo

    def send_products(inbox, outbox, at, vectors, line):
        mine = stacked(vectors)
        for q in range(n_plane // 2):
            both = fold(dot_nn(mine, kmat_ref[q]))
            for half in range(2):
                t = 2 * q + 1 + half
                block = both[:, half * own : (half + 1) * own]
                slot, where = (inbox, in_plane) if t == n_plane else (outbox, t - 1)
                slot[where, 0:cols, :] = block
                if line is not None:
                    slot[where, cols : cols + 1, :] = line
                if t < n_plane:
                    remote(outbox.at[where], inbox.at[in_plane], at, plane_peers[t - 1]).start()

    def products(inbox, at):
        all_plane(inbox, at).wait_recv()
        return total(inbox, 0, n_plane)

    all_line(extra_ref.at[0], 6).wait_recv()
    leaf_lanes = of_line(0, 0)
    parts, stat = by_subtree(0)
    lanes = leaf_lanes + expand(own_coef(parts))
    send_products(prod_ref, out_ref, 11, lanes, None)
    direction = pick(lanes)
    rz_now = to_col(stat) + level_product(parts)

    image = products(prod_ref, 11) + noise_level * direction
    put(1, image, dots(direction, image))
    send_line(line_ref.at[1], 1)
    leaf_image = leaf(image)
    send_extra(1, leaf_image, image)
    cross(1)
    all_line(extra_ref.at[1], 7).wait_recv()
    leaf_step = of_line(1, 0)
    sums, stat = by_subtree(1)
    alpha_0 = rz_now / to_col(stat)
    parts = [a - alpha_0 * s for a, s in zip(parts, sums)]
    leaf_lanes = leaf_lanes - alpha_0 * leaf_step
    residual_lanes = of_line(0, 1) - alpha_0 * of_line(1, 1)
    leaf_line = to_row(dots(residual_lanes, leaf_lanes))
    lanes = leaf_lanes + expand(own_coef(parts))
    send_products(prod_stat_ref, out_stat_ref, 12, lanes, leaf_line)
    answer = alpha_0 * direction
    residual = rhs - alpha_0 * image
    leaf_res = leaf_res - alpha_0 * leaf_image
    precond = pick(lanes)
    levels = level_product(parts)

    product = products(prod_stat_ref, 12)
    leaf_total = to_col(product[cols:])
    rz_next = leaf_total + levels
    beta_0 = rz_next / rz_now
    rz_now = rz_next
    direction = precond + beta_0 * direction
    image = product[0:cols] + noise_level * precond + beta_0 * image
    leaf_image = leaf(image)
    put(2, image, dots(direction, image), dots(image, leaf_res), dots(image, leaf_image))
    send_line(line_ref.at[2], 2)
    cross(2)
    sums, stat = by_subtree(2)
    alpha_1 = rz_now / to_col(stat)
    sol_ref[...] = answer + alpha_1 * direction
    res_ref[...] = residual - alpha_1 * image
    leaf_last = leaf_total - alpha_1 * (2.0 * to_col(stat, 1) - alpha_1 * to_col(stat, 2))
    parts = [a - alpha_1 * s for a, s in zip(parts, sums)]
    beta_1 = (leaf_last + level_product(parts)) / rz_now
    for i, (alpha, beta) in enumerate(((alpha_0, beta_0), (alpha_1, beta_1))):
        coef_ref[0, i : i + 1, :] = to_row(alpha)[:, 0:cols]
        coef_ref[1, i : i + 1, :] = to_row(beta)[:, 0:cols]
    for at in range(3):
        all_line(line_ref.at[at], at).wait_send()
        all_plane(plane_ref.at[at], 3 + at).wait_send()
    for at in range(2):
        all_line(extra_ref.at[at], 6 + at).wait_send()
    all_line(pts_line_ref, 8).wait_send()
    all_plane(pts_plane_ref, 9).wait_send()
    all_line(basis_ref, 10).wait_send()
    all_plane(prod_ref, 11).wait_send()
    all_plane(prod_stat_ref, 12).wait_send()


def on_device(n_row, n_col, points, inverse_length, target, probe_bits, leaf_inverse, top_basis, sub_basis):
    low = math.gcd(n_col, 8)
    n_line, n_plane = low, n_row * (n_col // low)
    dim, own = points.shape
    cols = probe_bits.shape[0] + 1
    rank = top_basis.shape[0]
    vmem = pl.BlockSpec(memory_space=pltpu.VMEM)
    hbm = pl.BlockSpec(memory_space=pltpu.HBM)
    return pl.pallas_call(
        functools.partial(kernel, n_row, n_col, low, rank),
        out_shape=(
            jax.ShapeDtypeStruct((cols, own), F32),
            jax.ShapeDtypeStruct((cols, own), F32),
            jax.ShapeDtypeStruct((2, ITERS, cols), F32),
        ),
        in_specs=[hbm] * 7,
        out_specs=(vmem, vmem, vmem),
        scratch_shapes=[
            pltpu.VMEM(points.shape, F32),
            pltpu.VMEM((1, dim), F32),
            pltpu.VMEM(probe_bits.shape, jnp.int32),
            pltpu.VMEM(leaf_inverse.shape, F32),
            pltpu.VMEM((n_line, 2 * rank, own), F32),
            pltpu.VMEM((2 * rank, 2 * n_line * own), BF16),
            pltpu.VMEM((1, own), F32),
            pltpu.VMEM((cols, own), F32),
            pltpu.VMEM((n_line, dim, own), F32),
            pltpu.VMEM((n_plane, dim, own), F32),
            pltpu.VMEM((3, n_line, cols + 1, own), F32),
            pltpu.VMEM((2, n_line, 2 * cols, own), F32),
            pltpu.VMEM((3, n_plane, cols + 1, own), F32),
            pltpu.VMEM((n_plane, cols, own), F32),
            pltpu.VMEM((n_plane, cols + 1, own), F32),
            pltpu.VMEM((n_plane - 1, cols, own), F32),
            pltpu.VMEM((n_plane - 1, cols + 1, own), F32),
            pltpu.VMEM((n_plane // 2, n_line * own, 4 * own), BF16),
            pltpu.SemaphoreType.DMA((7,)),
            pltpu.SemaphoreType.DMA((13,)),
            pltpu.SemaphoreType.DMA((13,)),
            pltpu.SemaphoreType.DMA((n_plane,)),
        ],
        compiler_params=pltpu.CompilerParams(
            collective_id=0, has_side_effects=True, vmem_limit_bytes=55202 * 1024
        ),
    )(
        points,
        inverse_length.reshape(1, dim),
        target.reshape(1, own),
        probe_bits,
        leaf_inverse,
        top_basis,
        sub_basis,
    )


def solution(mesh):
    return jax.shard_map(
        functools.partial(on_device, mesh.shape["row"], mesh.shape["col"]),
        mesh=mesh,
        in_specs=(
            P(None, ("row", "col")),
            P(),
            P(("row", "col")),
            P(None, ("row", "col")),
            P(("row", "col"), None),
            P(None, ("row", "col")),
            P(None, ("row", "col")),
        ),
        out_specs=(P(None, ("row", "col")), P(None, ("row", "col")), P()),
        check_vma=False,
    )
```
